32 devices in a mesh: dom: 4 (over z), rows: 8 (over y, x, core).
Axes of the slice: x: 2, y: 2, z: 4, core: 2. Of those that a mesh axis runs over, the one named last changes fastest.
Arguments:
- blocks: bfloat16 [512, 6, 128, 128], P('rows'), may hold values from -0.15625 to 0.15625
- columns: int32 [512, 6], P('rows'), may hold values from 0 to 511, as said below
- counts: int32 [8], P('rows'), may hold values from 2 to 64, as said below
- start_block: float32 [512, 2, 32, 128], P('rows'), may hold values from -6 to 6
- shift_radius: float32 [8], P('dom'), parts along dimension 0, may hold values from 1 to 1.25
- shift_angle: float32 [8], P('dom'), parts along dimension 0, may hold values from -3.140625 to 3.140625
Outputs:
- solution: float32 [2048, 2, 64, 128], P(('dom', 'rows')), parts along dimension 0
The draws below stay inside these ranges and needn't reach their ends.
There are 4 independent parts, one for each index of `dom`. The reference program is written for one: setup_inputs(seed, part) draws one part's arguments, and reference() takes and returns one part's arrays. A program takes and returns all parts, laid end to end along the dimension named above; an argument that names none is the same for every part. Nothing has to cross between parts.
Inputs may be any that keep to these rules, and one draw needn't show every extreme that they name: `counts`: live block-rows of each device; some device has all 64 live. `columns`: A live block-row i of device d lists first i itself, then three live block-rows of d, then two block-rows among the first 2 of devices other than d. A dead block-row lists only itself.
All inputs are finite; a program needn't handle non-finite values.
Results may differ from the reference program's by a relative error of at most 0.0038.
Values may be sent and summed in bfloat16 or wider, within the bound.
A program may use at most 128 MiB of HBM per device.

```python
import math
import jax
import jax.numpy as jnp

BS = 128
NNZB = 6
NVEC = 16
SHIFTS = 2
HB = 2
ITERS = 4
CAP = 64
OWNERS = 8
NBR = 512


def structure(key):
    spread = CAP - HB
    first_draw = jax.random.randint(jax.random.fold_in(key, 101), (OWNERS,), 0, spread + 1)
    second = jax.random.randint(jax.random.fold_in(key, 102), (OWNERS,), 0, spread + 1)
    counts = HB + first_draw * second // spread
    chosen = jax.random.randint(jax.random.fold_in(key, 103), (), 0, OWNERS)
    counts = jnp.where(jnp.arange(OWNERS) == chosen, CAP, counts).astype(jnp.int32)
    row_ids = jnp.arange(NBR, dtype=jnp.int32)
    owner_dev = row_ids // CAP
    slot_pos = row_ids % CAP
    alive_count = counts[owner_dev]
    near_cols = jax.random.randint(jax.random.fold_in(key, 104), (NBR, 3), 0, 1 << 20) % alive_count[:, None] + owner_dev[:, None] * CAP
    hop_count = jax.random.randint(jax.random.fold_in(key, 105), (NBR, 2), 1, OWNERS)
    hop_first = jnp.where(slot_pos == 1, 1, hop_count[:, 0])
    hop_second = jnp.where(slot_pos == 0, OWNERS // 2, hop_count[:, 1])
    hop_count = jnp.stack([hop_first, hop_second], 1)
    far_dev = (owner_dev[:, None] + hop_count) % OWNERS
    far_slot = jax.random.randint(jax.random.fold_in(key, 106), (NBR, 2), 0, HB)
    far_cols = far_dev * CAP + far_slot
    listed = jnp.concatenate([row_ids[:, None], near_cols, far_cols], 1)
    listed = jnp.where((slot_pos < alive_count)[:, None], listed, row_ids[:, None])
    return (counts, listed.astype(jnp.int32))


def draw_columns(key, part):
    return structure(key)[1]


def draw_counts(key, part):
    return structure(key)[0]


def block_levels(rng, dims, shards, least, top_value):
    level = 1.0
    for dim, blocks in shards:
        heights = jax.random.uniform(jax.random.fold_in(jax.random.fold_in(rng, 6), dim), (blocks,), jnp.float32, least / len(shards), top_value / len(shards))
        level = level * jnp.repeat(jnp.exp(heights), dims[dim] // blocks).reshape((-1,) + (1,) * (len(dims) - 1 - dim))
    return level


def centred(stream_key, dims, scale, limit, pieces=(), kind=jnp.bfloat16):
    entries = scale * jax.random.normal(stream_key, dims, jnp.float32)
    if pieces:
        entries = entries * block_levels(stream_key, dims, pieces, -0.22, 0.18)
    return jnp.clip(entries, -limit, limit).astype(kind)


def setup_inputs(seed: int = 0, part: int = 0) -> dict:
    keys = jax.random.split(jax.random.key(seed), 7)
    part_keys = jax.random.split(jax.random.fold_in(keys[6], part), 7)
    blocks = centred(keys[0], (NBR, NNZB, BS, BS), (2 * NNZB * BS) ** -0.5, 0.15625, ((0, 8),))
    columns = draw_columns(jax.random.fold_in(keys[6], 71), part)
    counts = draw_counts(jax.random.fold_in(keys[6], 71), part)
    start_block = centred(keys[3], (NBR, 2, 2 * NVEC, BS), 1.0, 6.0, ((0, 8),), jnp.float32)
    shift_radius = jnp.clip(jnp.exp(jax.random.uniform(part_keys[4], (SHIFTS,), jnp.float32, math.log(1.0), math.log(1.25))), 1.0, 1.25)
    shift_angle = jnp.clip(jax.random.uniform(part_keys[5], (SHIFTS,), jnp.float32, -3.140625, 3.140625), -3.140625, 3.140625)
    return dict(blocks=blocks, columns=columns, counts=counts, start_block=start_block, shift_radius=shift_radius, shift_angle=shift_angle)


def rotate(values, weight_re, weight_im):
    row_count = values.shape[0]
    grouped = values.reshape(row_count, 2, weight_re.shape[0], 2, -1, values.shape[-1])
    real_part = grouped[:, :, :, 0]
    imag_part = grouped[:, :, :, 1]
    scale_re = weight_re[None, None, :, None, None]
    scale_im = weight_im[None, None, :, None, None]
    out_re = scale_re * real_part - scale_im * imag_part
    out_im = scale_re * imag_part + scale_im * real_part
    return jnp.stack([out_re, out_im], 3).reshape(values.shape)


def reference(blocks, columns, counts, start_block, shift_radius, shift_angle):
    block_rows = blocks.shape[0]
    row_ids = jnp.arange(block_rows, dtype=jnp.int32)
    owner_dev = row_ids // CAP
    alive_rows = ((row_ids % CAP) < counts[owner_dev]).astype(jnp.float32)
    source = start_block * alive_rows[:, None, None, None]
    width = start_block.shape[-1]
    driven = jnp.broadcast_to(source[:, :, None], (block_rows, 2, SHIFTS, 2 * NVEC, width)).reshape(block_rows, 2, SHIFTS * 2 * NVEC, width)
    weight_re = jnp.cos(shift_angle) / shift_radius
    weight_im = -jnp.sin(shift_angle) / shift_radius
    tiles = blocks.astype(jnp.float32)
    iterate = rotate(driven, weight_re, weight_im)
    for counter in range(ITERS):
        packed = iterate.astype(jnp.bfloat16).astype(jnp.float32)
        upper_half = packed[:, 0]
        lower_half = packed[:, 1]
        picked = lower_half[columns]
        top_part = jnp.einsum("knab,kncb->kca", tiles, picked) * alive_rows[:, None, None]
        partial_terms = jnp.einsum("knab,kca->kncb", tiles, upper_half)
        bottom = jax.ops.segment_sum(partial_terms.reshape(-1, partial_terms.shape[2], width), columns.reshape(-1), num_segments=block_rows)
        iterate = rotate(driven + jnp.stack([top_part, bottom], 1), weight_re, weight_im)
    return iterate
```

```python
import functools

import jax
import jax.numpy as jnp
from jax import lax
from jax.experimental import pallas as pl
from jax.experimental.pallas import tpu as pltpu
from jax.sharding import PartitionSpec as P

HB = 2
ITERS = 4
NEAR = 4
F32 = jnp.float32
BF16 = jnp.bfloat16


def pick_unroll(total, want):
    while total % want:
        want -= 1
    return want


def kernel(
    n, slots, far, nvec, shifts,
    meta, weight, blocks, start, out,
    near_w, far_w, drive, upper, lower, near_sum, far_sum,
    send_terms, heads, far_heads, terms, out_u, out_l,
    load_sem, out_sem, head_send, head_recv, term_send, term_recv,
):
    me = lax.axis_index("rows")
    near_total = slots * (NEAR - 1)
    far_total = slots * far
    far_rows = (n - 1) * HB
    at_far_keep = far_total
    at_near = 2 * far_total
    at_near_keep = at_near + near_total
    at_far_last = at_near_keep + near_total
    at_near_last = at_far_last + far_rows
    at_near_col = at_near_last + slots
    at_far_col = at_near_col + near_total
    at_count = at_far_col + far_total

    load_start = pltpu.make_async_copy(start, drive, load_sem.at[0])
    load_far = pltpu.make_async_copy(blocks.at[:, NEAR:], far_w, load_sem.at[1])
    load_near = pltpu.make_async_copy(blocks.at[:, :NEAR], near_w, load_sem.at[2])
    load_start.start()
    load_far.start()
    load_near.start()

    barrier = pltpu.get_barrier_semaphore()
    for off in range(1, n):
        pl.semaphore_signal(
            barrier, inc=1, device_id={"rows": lax.rem(me + off, n)},
            device_id_type=pl.DeviceIdType.MESH,
        )

    def rotated(values):
        pieces = []
        for s in range(shifts):
            re = values[(2 * s) * nvec:(2 * s + 1) * nvec]
            im = values[(2 * s + 1) * nvec:(2 * s + 2) * nvec]
            w_re = weight[s]
            w_im = weight[shifts + s]
            pieces.append(w_re * re - w_im * im)
            pieces.append(w_re * im + w_im * re)
        return jnp.concatenate(pieces, 0)

    def driven(k, half):
        return jnp.concatenate([drive[k, half]] * shifts, 0)

    load_start.wait()

    def begin(k, carry):
        alive = (k < meta[at_count]).astype(F32)
        drive[k] = drive[k] * alive
        upper[0, k] = rotated(driven(k, 0)).astype(BF16)
        lower[0, k] = rotated(driven(k, 1)).astype(BF16)
        return carry

    lax.fori_loop(0, slots, begin, 0, unroll=2)
    near_sum[0] = jnp.zeros(near_sum.shape[1:], near_sum.dtype)
    far_sum[0] = jnp.zeros(far_sum.shape[1:], far_sum.dtype)
    pl.semaphore_wait(barrier, n - 1)

    def head_copy(p, off):
        return pltpu.make_async_remote_copy(
            src_ref=lower.at[p, pl.ds(0, HB)],
            dst_ref=heads.at[p, pl.ds((n - off - 1) * HB, HB)],
            send_sem=head_send.at[off - 1],
            recv_sem=head_recv.at[p, n - off - 1],
            device_id={"rows": lax.rem(me + off, n)},
            device_id_type=pl.DeviceIdType.MESH,
        )

    def term_copy(p, off):
        return pltpu.make_async_remote_copy(
            src_ref=send_terms.at[pl.ds((off - 1) * HB, HB)],
            dst_ref=terms.at[p, pl.ds((n - off - 1) * HB, HB)],
            send_sem=term_send.at[off - 1],
            recv_sem=term_recv.at[p, n - off - 1],
            device_id={"rows": lax.rem(me + off, n)},
            device_id_type=pl.DeviceIdType.MESH,
        )

    def dot(a, b):
        return jnp.dot(a, b, preferred_element_type=F32)

    def sweep(s, last):
        p = lax.rem(s, 2)
        q = 1 - p
        for off in range(1, n):
            head_copy(p, off).start()

        step_far = pick_unroll(far_total, 32)

        def far_step(i, acc):
            for u in range(step_far):
                j = i * step_far + u
                e = meta[j]
                keep = meta[at_far_keep + j].astype(F32)
                k = e // far
                acc = acc * keep + dot(upper[p, k], far_w[k, e - k * far])
                far_sum[j + 1] = acc.astype(BF16)
            return acc

        zero = jnp.zeros(upper.shape[2:], F32)
        lax.fori_loop(0, far_total // step_far, far_step, zero)
        for off in range(1, n):
            for h in range(HB):
                row = (off - 1) * HB + h
                send_terms[row] = far_sum[meta[at_far_last + row]]
            term_copy(p, off).start()

        step_near = pick_unroll(near_total, 32)

        def near_step(i, acc):
            for u in range(step_near):
                j = i * step_near + u
                e = meta[at_near + j]
                keep = meta[at_near_keep + j].astype(F32)
                k = e // NEAR
                acc = acc * keep + dot(upper[p, k], near_w[k, e - k * NEAR])
                near_sum[j + 1] = acc
            return acc

        lax.fori_loop(0, near_total // step_near, near_step, zero)

        for off in range(1, n):
            head_copy(p, off).wait_recv()
        for row in range(far_rows):
            far_heads[row] = heads[p, row]

        step_top = pick_unroll(slots, 8)

        def top_step(i, carry):
            for u in range(step_top):
                k = i * step_top + u
                tiles = [lower[p, k]]
                for c in range(NEAR - 1):
                    tiles.append(lower[p, meta[at_near_col + k * (NEAR - 1) + c]])
                for c in range(far):
                    tiles.append(far_heads[meta[at_far_col + k * far + c]])
                rhs = [near_w[k, c] for c in range(NEAR)] + [far_w[k, c] for c in range(far)]
                got = lax.dot_general(
                    jnp.concatenate(tiles, 1), jnp.concatenate(rhs, 1),
                    (((1,), (1,)), ((), ())), preferred_element_type=F32,
                )
                alive = (k < meta[at_count]).astype(F32)
                value = rotated(driven(k, 0) + got * alive)
                if last:
                    out_u[k] = value
                else:
                    upper[q, k] = value.astype(BF16)
            return carry

        lax.fori_loop(0, slots // step_top, top_step, 0)
        if last:
            write_u.start()

        for off in range(1, n):
            term_copy(p, off).wait_recv()

        def bottom(k, extra):
            value = driven(k, 1) + dot(upper[p, k], near_w[k, 0])
            value = value + near_sum[meta[at_near_last + k]]
            for row in range(extra):
                value = value + terms[p, row * HB + k].astype(F32)
            value = rotated(value)
            if last:
                out_l[k] = value
            else:
                lower[q, k] = value.astype(BF16)

        for k in range(HB):
            bottom(k, n - 1)
        step_bottom = pick_unroll(slots - HB, 31)

        def bottom_step(i, carry):
            for u in range(step_bottom):
                bottom(HB + i * step_bottom + u, 0)
            return carry

        lax.fori_loop(0, (slots - HB) // step_bottom, bottom_step, 0)
        if last:
            write_l.start()
        for off in range(1, n):
            head_copy(p, off).wait_send()
            term_copy(p, off).wait_send()

    write_u = pltpu.make_async_copy(out_u, out.at[:, 0], out_sem.at[0])
    write_l = pltpu.make_async_copy(out_l, out.at[:, 1], out_sem.at[1])
    load_far.wait()
    load_near.wait()

    def middle(s, carry):
        sweep(s, False)
        return carry

    lax.fori_loop(0, ITERS - 1, middle, 0)
    sweep(ITERS - 1, True)
    write_u.wait()
    write_l.wait()


def plan(columns, counts, me, n):
    slots, stored = columns.shape
    far = stored - NEAR
    owner = columns // slots
    within = columns - owner * slots
    rel = lax.rem(owner - me + n, n)
    near_col = within[:, 1:NEAR].reshape(-1)
    far_rows = (n - 1) * HB
    far_col = jnp.clip((rel - 1) * HB + within, 0, far_rows - 1)[:, NEAR:].reshape(-1)
    dest = jnp.concatenate([far_col, far_rows + near_col])
    total = dest.shape[0]
    far_total = far_col.shape[0]
    here = jnp.arange(total, dtype=jnp.int32)
    near_entry = here - far_total
    near_row = near_entry // (NEAR - 1)
    entry = jnp.where(
        here < far_total, here, near_row * NEAR + 1 + near_entry - near_row * (NEAR - 1)
    )
    key = dest * total + here
    rank = jnp.sum((key[None, :] < key[:, None]).astype(jnp.int32), 1)
    hit = rank[None, :] == here[:, None]
    perm = jnp.sum(jnp.where(hit, entry[None, :], 0), 1)
    dest_sorted = jnp.sum(jnp.where(hit, dest[None, :], 0), 1)
    previous = jnp.sum(jnp.where(rank[None, :] == here[:, None] - 1, dest[None, :] + 1, 0), 1)
    keep = (previous == dest_sorted + 1).astype(jnp.int32)
    keep = jnp.where(here == far_total, 0, keep)
    rows = jnp.arange(far_rows + slots, dtype=jnp.int32)
    ends = jnp.sum((dest[None, :] <= rows[:, None]).astype(jnp.int32), 1)
    some = jnp.sum((dest[None, :] == rows[:, None]).astype(jnp.int32), 1)
    ends = ends - jnp.where(rows >= far_rows, far_total, 0)
    ends = jnp.where(some > 0, ends, 0)
    return jnp.concatenate([
        perm[:far_total], keep[:far_total], perm[far_total:], keep[far_total:],
        ends, near_col, far_col, counts,
    ])


def body(blocks, columns, counts, start_block, shift_radius, shift_angle):
    me = lax.axis_index("rows")
    n = lax.axis_size("rows")
    slots, stored, width = blocks.shape[0], blocks.shape[1], blocks.shape[-1]
    far = stored - NEAR
    shifts = shift_radius.shape[0]
    two_nvec = start_block.shape[2]
    cols = shifts * two_nvec
    meta = plan(columns, counts, me, n)
    weight = jnp.concatenate(
        [jnp.cos(shift_angle) / shift_radius, -jnp.sin(shift_angle) / shift_radius]
    )
    far_rows = (n - 1) * HB
    near_total = slots * (NEAR - 1)
    far_total = slots * far
    flops = ITERS * 4 * slots * stored * width * width * cols
    smem = pl.BlockSpec(memory_space=pltpu.SMEM)
    hbm = pl.BlockSpec(memory_space=pl.ANY)
    return pl.pallas_call(
        functools.partial(kernel, n, slots, far, two_nvec // 2, shifts),
        out_shape=jax.ShapeDtypeStruct((slots, 2, cols, width), F32),
        in_specs=[smem, smem, hbm, hbm],
        out_specs=hbm,
        scratch_shapes=[
            pltpu.VMEM((slots, NEAR, width, width), BF16),
            pltpu.VMEM((slots, far, width, width), BF16),
            pltpu.VMEM(start_block.shape, F32),
            pltpu.VMEM((2, slots, cols, width), BF16),
            pltpu.VMEM((2, slots, cols, width), BF16),
            pltpu.VMEM((near_total + 1, cols, width), F32),
            pltpu.VMEM((far_total + 1, cols, width), BF16),
            pltpu.VMEM((far_rows, cols, width), BF16),
            pltpu.VMEM((2, far_rows, cols, width), BF16),
            pltpu.VMEM((far_rows, cols, width), BF16),
            pltpu.VMEM((2, far_rows, cols, width), BF16),
            pltpu.VMEM((slots, cols, width), F32),
            pltpu.VMEM((slots, cols, width), F32),
            pltpu.SemaphoreType.DMA((3,)),
            pltpu.SemaphoreType.DMA((2,)),
            pltpu.SemaphoreType.DMA((n - 1,)),
            pltpu.SemaphoreType.DMA((2, n - 1)),
            pltpu.SemaphoreType.DMA((n - 1,)),
            pltpu.SemaphoreType.DMA((2, n - 1)),
        ],
        compiler_params=pltpu.CompilerParams(
            collective_id=0, has_side_effects=True, vmem_limit_bytes=56 * 1024 * 1024
        ),
        cost_estimate=pl.CostEstimate(
            flops=flops, bytes_accessed=2 * blocks.size, transcendentals=0
        ),
    )(meta, weight, blocks, start_block)


def solution(mesh):
    placed = (
        P("rows", None, None, None),
        P("rows", None),
        P("rows"),
        P("rows", None, None, None),
        P("dom"),
        P("dom"),
    )
    return jax.shard_map(
        body,
        mesh=mesh,
        in_specs=placed,
        out_specs=P(("dom", "rows"), None, None, None),
        check_vma=False,
    )
```

```python
import functools

import jax
import jax.numpy as jnp
from jax import lax
from jax.experimental import pallas as pl
from jax.experimental.pallas import tpu as pltpu
from jax.sharding import PartitionSpec as P

HB = 2
ITERS = 4
NEAR = 4
F32 = jnp.float32
BF16 = jnp.bfloat16


def pick_unroll(total, want):
    while total % want:
        want -= 1
    return want


def pair_counts(slots, far, n):
    far_rows = (n - 1) * HB
    far_pairs = (slots * far + far_rows) // 2
    near_pairs = (slots * NEAR + slots) // 2
    return -(-far_pairs // 8) * 8, -(-near_pairs // 8) * 8


def split(entry, width):
    if width & (width - 1):
        k = lax.div(entry, jnp.int32(width))
        return k, entry - k * width
    shift = width.bit_length() - 1
    return lax.shift_right_logical(entry, jnp.int32(shift)), entry & (width - 1)


def kernel(
    n, slots, far, nvec, shifts,
    meta, weight, blocks, start, out,
    near_w, far_w, drive, upper, lower, near_sum, far_sum,
    send_terms, heads, far_heads, terms, out_u, out_l,
    load_sem, out_sem, head_send, head_recv, term_send, term_recv,
):
    me = lax.axis_index("rows")
    near_total = slots * (NEAR - 1)
    far_total = slots * far
    far_rows = (n - 1) * HB
    far_pairs, near_pairs = pair_counts(slots, far, n)
    at_keep = 2 * (far_pairs + near_pairs)
    at_far_last = at_keep + far_pairs + near_pairs
    at_near_last = at_far_last + far_rows
    at_near_col = at_near_last + slots
    at_far_col = at_near_col + near_total
    at_count = at_far_col + far_total

    load_start = pltpu.make_async_copy(start, drive, load_sem.at[0])
    load_far = pltpu.make_async_copy(blocks.at[:, NEAR:], far_w.at[pl.ds(0, slots)], load_sem.at[1])
    load_near = pltpu.make_async_copy(blocks.at[:, :NEAR], near_w.at[pl.ds(0, slots)], load_sem.at[2])
    load_start.start()
    load_far.start()
    load_near.start()

    barrier = pltpu.get_barrier_semaphore()
    for off in range(1, n):
        pl.semaphore_signal(
            barrier, inc=1, device_id={"rows": lax.rem(me + off, n)},
            device_id_type=pl.DeviceIdType.MESH,
        )

    def rotated(values):
        pieces = []
        for s in range(shifts):
            re = values[(2 * s) * nvec:(2 * s + 1) * nvec]
            im = values[(2 * s + 1) * nvec:(2 * s + 2) * nvec]
            w_re = weight[s]
            w_im = weight[shifts + s]
            pieces.append(w_re * re - w_im * im)
            pieces.append(w_re * im + w_im * re)
        return jnp.concatenate(pieces, 0)

    def driven(k, half):
        return jnp.concatenate([drive[k, half]] * shifts, 0)

    load_start.wait()

    def begin(k, carry):
        alive = (k < meta[at_count]).astype(F32)
        drive[k] = drive[k] * alive
        upper[0, k] = rotated(driven(k, 0)).astype(BF16)
        lower[0, k] = rotated(driven(k, 1)).astype(BF16)
        return carry

    lax.fori_loop(0, slots, begin, 0, unroll=2)
    for p in range(2):
        upper[p, slots] = jnp.zeros(upper.shape[2:], upper.dtype)
    near_w[slots, 0] = jnp.zeros(near_w.shape[2:], near_w.dtype)
    far_w[slots, 0] = jnp.zeros(far_w.shape[2:], far_w.dtype)
    near_sum[0] = jnp.zeros(near_sum.shape[1:], near_sum.dtype)
    far_sum[0] = jnp.zeros(far_sum.shape[1:], far_sum.dtype)
    pl.semaphore_wait(barrier, n - 1)

    def head_copy(p, off):
        return pltpu.make_async_remote_copy(
            src_ref=lower.at[p, pl.ds(0, HB)],
            dst_ref=heads.at[p, pl.ds((n - off - 1) * HB, HB)],
            send_sem=head_send.at[off - 1],
            recv_sem=head_recv.at[p, n - off - 1],
            device_id={"rows": lax.rem(me + off, n)},
            device_id_type=pl.DeviceIdType.MESH,
        )

    def term_copy(p, off):
        return pltpu.make_async_remote_copy(
            src_ref=send_terms.at[pl.ds((off - 1) * HB, HB)],
            dst_ref=terms.at[p, pl.ds((n - off - 1) * HB, HB)],
            send_sem=term_send.at[off - 1],
            recv_sem=term_recv.at[p, n - off - 1],
            device_id={"rows": lax.rem(me + off, n)},
            device_id_type=pl.DeviceIdType.MESH,
        )

    def dot(a, b):
        return jnp.dot(a, b, preferred_element_type=F32)

    def sweep(s, last):
        p = lax.rem(s, 2)
        q = 1 - p
        for off in range(1, n):
            head_copy(p, off).start()

        zero = jnp.zeros(upper.shape[2:], F32)

        def running(first, pairs, blocks_of, weights, sums):
            step = pick_unroll(pairs, 24)
            group = pick_unroll(step, 8)

            def go(i, acc):
                for g in range(step // group):
                    found = []
                    for u in range(group):
                        j = i * step + g * group + u
                        lhs, rhs = [], []
                        for side in range(2):
                            e = meta[2 * (first + j) + side]
                            k, c = split(e, blocks_of)
                            lhs.append(upper[p, k])
                            rhs.append(weights[k, c])
                        found.append(dot(jnp.concatenate(lhs, 1), jnp.concatenate(rhs, 0)))
                    for u in range(group):
                        j = i * step + g * group + u
                        acc = acc * meta[at_keep + first + j].astype(F32) + found[u]
                        sums[j + 1] = acc.astype(sums.dtype)
                return acc

            lax.fori_loop(0, pairs // step, go, zero)

        running(0, far_pairs, far, far_w, far_sum)
        for off in range(1, n):
            for h in range(HB):
                row = (off - 1) * HB + h
                send_terms[row] = far_sum[meta[at_far_last + row]]
            term_copy(p, off).start()
        running(far_pairs, near_pairs, NEAR, near_w, near_sum)

        def bottom(k, extra):
            value = driven(k, 1) + near_sum[meta[at_near_last + k]]
            for row in range(extra):
                value = value + terms[p, row * HB + k].astype(F32)
            value = rotated(value)
            if last:
                out_l[k] = value
            else:
                lower[q, k] = value.astype(BF16)

        def bottom_step(k, carry):
            bottom(k, 0)
            return carry

        lax.fori_loop(HB, slots, bottom_step, 0, unroll=4)

        for off in range(1, n):
            head_copy(p, off).wait_recv()
        for row in range(far_rows):
            far_heads[row] = heads[p, row]

        step_top = pick_unroll(slots, 8)
        group_top = pick_unroll(step_top, 4)

        def top_step(i, carry):
            for g in range(step_top // group_top):
                found = []
                for u in range(group_top):
                    k = i * step_top + g * group_top + u
                    tiles = [lower[p, k]]
                    for c in range(NEAR - 1):
                        tiles.append(lower[p, meta[at_near_col + k * (NEAR - 1) + c]])
                    for c in range(far):
                        tiles.append(far_heads[meta[at_far_col + k * far + c]])
                    rhs = [near_w[k, c] for c in range(NEAR)] + [far_w[k, c] for c in range(far)]
                    found.append(lax.dot_general(
                        jnp.concatenate(tiles, 1), jnp.concatenate(rhs, 1),
                        (((1,), (1,)), ((), ())), preferred_element_type=F32,
                    ))
                for u in range(group_top):
                    k = i * step_top + g * group_top + u
                    alive = (k < meta[at_count]).astype(F32)
                    value = rotated(driven(k, 0) + found[u] * alive)
                    if last:
                        out_u[k] = value
                    else:
                        upper[q, k] = value.astype(BF16)
            return carry

        lax.fori_loop(0, slots // step_top, top_step, 0)
        if last:
            write_u.start()

        for off in range(1, n):
            term_copy(p, off).wait_recv()
        for k in range(HB):
            bottom(k, n - 1)
        if last:
            write_l.start()
        for off in range(1, n):
            head_copy(p, off).wait_send()
            term_copy(p, off).wait_send()

    write_u = pltpu.make_async_copy(out_u, out.at[:, 0], out_sem.at[0])
    write_l = pltpu.make_async_copy(out_l, out.at[:, 1], out_sem.at[1])
    load_far.wait()
    load_near.wait()

    def middle(s, carry):
        sweep(s, False)
        return carry

    lax.fori_loop(0, ITERS - 1, middle, 0)
    sweep(ITERS - 1, True)
    write_u.wait()
    write_l.wait()


def plan(columns, counts, me, n):
    slots, stored = columns.shape
    far = stored - NEAR
    owner = columns // slots
    within = columns - owner * slots
    rel = lax.rem(owner - me + n, n)
    far_rows = (n - 1) * HB
    far_pairs, near_pairs = pair_counts(slots, far, n)
    near_all = within[:, :NEAR].reshape(-1)
    far_col = jnp.clip((rel - 1) * HB + within, 0, far_rows - 1)[:, NEAR:].reshape(-1)
    far_total = far_col.shape[0]
    dest = jnp.concatenate([far_col, far_rows + near_all])
    here = jnp.arange(dest.shape[0], dtype=jnp.int32)
    entry = jnp.where(here < far_total, here, here - far_total)
    rows = jnp.arange(far_rows + slots, dtype=jnp.int32)
    same = dest[None, :] == dest[:, None]
    order = jnp.sum((same & (here[None, :] < here[:, None])).astype(jnp.int32), 1)
    even = 1 - (order & 1)
    is_near = (rows >= far_rows).astype(jnp.int32)
    dest_near = (dest >= far_rows).astype(jnp.int32)
    ahead_rows = is_near * far_pairs + jnp.sum(
        jnp.where((dest[None, :] < rows[:, None]) & (dest_near[None, :] == is_near[:, None]),
                  even[None, :], 0), 1)
    own_rows = jnp.sum(jnp.where(dest[None, :] == rows[:, None], even[None, :], 0), 1)
    ahead = dest_near * far_pairs + jnp.sum(
        jnp.where((dest[None, :] < dest[:, None]) & (dest_near[None, :] == dest_near[:, None]),
                  even[None, :], 0), 1)
    place = 2 * ahead + order
    pairs = far_pairs + near_pairs
    spots = jnp.arange(2 * pairs, dtype=jnp.int32)
    empty = jnp.where(spots < 2 * far_pairs, slots * far, slots * NEAR)
    listed = jnp.sum(
        jnp.where(place[None, :] == spots[:, None], entry[None, :] - empty[:, None], 0), 1
    ) + empty
    pair_ids = jnp.arange(pairs, dtype=jnp.int32)
    starts = (ahead_rows[None, :] == pair_ids[:, None]) & (own_rows[None, :] > 0)
    keep = 1 - jnp.sum(starts.astype(jnp.int32), 1)
    ends = jnp.where(own_rows > 0, ahead_rows + own_rows - is_near * far_pairs, 0)
    return jnp.concatenate(
        [listed, keep, ends, within[:, 1:NEAR].reshape(-1), far_col, counts]
    )


def body(blocks, columns, counts, start_block, shift_radius, shift_angle):
    me = lax.axis_index("rows")
    n = lax.axis_size("rows")
    slots, stored, width = blocks.shape[0], blocks.shape[1], blocks.shape[-1]
    far = stored - NEAR
    shifts = shift_radius.shape[0]
    two_nvec = start_block.shape[2]
    cols = shifts * two_nvec
    meta = plan(columns, counts, me, n)
    weight = jnp.concatenate(
        [jnp.cos(shift_angle) / shift_radius, -jnp.sin(shift_angle) / shift_radius]
    )
    far_rows = (n - 1) * HB
    far_pairs, near_pairs = pair_counts(slots, far, n)
    flops = ITERS * 4 * slots * stored * width * width * cols
    smem = pl.BlockSpec(memory_space=pltpu.SMEM)
    hbm = pl.BlockSpec(memory_space=pl.ANY)
    return pl.pallas_call(
        functools.partial(kernel, n, slots, far, two_nvec // 2, shifts),
        out_shape=jax.ShapeDtypeStruct((slots, 2, cols, width), F32),
        in_specs=[smem, smem, hbm, hbm],
        out_specs=hbm,
        scratch_shapes=[
            pltpu.VMEM((slots + 1, NEAR, width, width), BF16),
            pltpu.VMEM((slots + 1, far, width, width), BF16),
            pltpu.VMEM(start_block.shape, F32),
            pltpu.VMEM((2, slots + 1, cols, width), BF16),
            pltpu.VMEM((2, slots, cols, width), BF16),
            pltpu.VMEM((near_pairs + 1, cols, width), F32),
            pltpu.VMEM((far_pairs + 1, cols, width), BF16),
            pltpu.VMEM((far_rows, cols, width), BF16),
            pltpu.VMEM((2, far_rows, cols, width), BF16),
            pltpu.VMEM((far_rows, cols, width), BF16),
            pltpu.VMEM((2, far_rows, cols, width), BF16),
            pltpu.VMEM((slots, cols, width), F32),
            pltpu.VMEM((slots, cols, width), F32),
            pltpu.SemaphoreType.DMA((3,)),
            pltpu.SemaphoreType.DMA((2,)),
            pltpu.SemaphoreType.DMA((n - 1,)),
            pltpu.SemaphoreType.DMA((2, n - 1)),
            pltpu.SemaphoreType.DMA((n - 1,)),
            pltpu.SemaphoreType.DMA((2, n - 1)),
        ],
        compiler_params=pltpu.CompilerParams(
            collective_id=0, has_side_effects=True, vmem_limit_bytes=56 * 1024 * 1024
        ),
        cost_estimate=pl.CostEstimate(
            flops=flops, bytes_accessed=2 * blocks.size, transcendentals=0
        ),
    )(meta, weight, blocks, start_block)


def solution(mesh):
    placed = (
        P("rows", None, None, None),
        P("rows", None),
        P("rows"),
        P("rows", None, None, None),
        P("dom"),
        P("dom"),
    )
    return jax.shard_map(
        body,
        mesh=mesh,
        in_specs=placed,
        out_specs=P(("dom", "rows"), None, None, None),
        check_vma=False,
    )
```

```python
import functools

import jax
import jax.numpy as jnp
from jax import lax
from jax.experimental import pallas as pl
from jax.experimental.pallas import tpu as pltpu
from jax.sharding import PartitionSpec as P

HB = 2
ITERS = 4
NEAR = 4
F32 = jnp.float32
BF16 = jnp.bfloat16


def pick_unroll(total, want):
    while total % want:
        want -= 1
    return want


def pair_counts(slots, far, n):
    far_rows = (n - 1) * HB
    far_pairs = (slots * far + far_rows) // 2
    near_pairs = (slots * NEAR + slots) // 2
    return -(-far_pairs // 8) * 8, -(-near_pairs // 8) * 8


def split(entry, width):
    if width & (width - 1):
        k = lax.div(entry, jnp.int32(width))
        return k, entry - k * width
    shift = width.bit_length() - 1
    return lax.shift_right_logical(entry, jnp.int32(shift)), entry & (width - 1)


def kernel(
    n, slots, far, nvec, shifts,
    meta, weight, blocks, start, out,
    near_w, far_w, turned, drive, upper, lower, near_sum, far_sum,
    send_terms, heads, far_heads, terms, out_u, out_l,
    load_sem, far_sem, near_sem, out_sem, head_send, head_recv, term_send, term_recv,
):
    me = lax.axis_index("rows")
    near_total = slots * (NEAR - 1)
    far_total = slots * far
    far_rows = (n - 1) * HB
    far_pairs, near_pairs = pair_counts(slots, far, n)
    at_keep = 2 * (far_pairs + near_pairs)
    at_far_last = at_keep + far_pairs + near_pairs
    at_near_last = at_far_last + far_rows
    at_near_col = at_near_last + slots
    at_far_col = at_near_col + near_total
    at_count = at_far_col + far_total

    load_start = pltpu.make_async_copy(start, drive, load_sem.at[0])
    chunk = pick_unroll(slots, 8)
    width = turned.shape[2]

    def load_far(i):
        rows = pl.ds(i * chunk, chunk)
        return pltpu.make_async_copy(blocks.at[rows, NEAR:], far_w.at[rows], far_sem.at[i])

    def load_near(i):
        rows = pl.ds(i * chunk, chunk)
        return pltpu.make_async_copy(blocks.at[rows, :NEAR], near_w.at[rows], near_sem.at[i])

    load_start.start()
    for i in range(slots // chunk):
        load_far(i).start()
        load_near(i).start()

    barrier = pltpu.get_barrier_semaphore()
    for off in range(1, n):
        pl.semaphore_signal(
            barrier, inc=1, device_id={"rows": lax.rem(me + off, n)},
            device_id_type=pl.DeviceIdType.MESH,
        )

    def rotated(values):
        pieces = []
        for s in range(shifts):
            re = values[(2 * s) * nvec:(2 * s + 1) * nvec]
            im = values[(2 * s + 1) * nvec:(2 * s + 2) * nvec]
            w_re = weight[s]
            w_im = weight[shifts + s]
            pieces.append(w_re * re - w_im * im)
            pieces.append(w_re * im + w_im * re)
        return jnp.concatenate(pieces, 0)

    def driven(k, half):
        return jnp.concatenate([drive[k, half]] * shifts, 0)

    load_start.wait()

    def begin(k, carry):
        alive = (k < meta[at_count]).astype(F32)
        drive[k] = drive[k] * alive
        upper[0, k] = rotated(driven(k, 0)).astype(BF16)
        lower[0, k] = rotated(driven(k, 1)).astype(BF16)
        return carry

    lax.fori_loop(0, slots, begin, 0, unroll=2)
    for p in range(2):
        upper[p, slots] = jnp.zeros(upper.shape[2:], upper.dtype)
    near_w[slots, 0] = jnp.zeros(near_w.shape[2:], near_w.dtype)
    far_w[slots, 0] = jnp.zeros(far_w.shape[2:], far_w.dtype)
    near_sum[0] = jnp.zeros(near_sum.shape[1:], near_sum.dtype)
    far_sum[0] = jnp.zeros(far_sum.shape[1:], far_sum.dtype)
    pl.semaphore_wait(barrier, n - 1)

    def head_copy(p, off):
        return pltpu.make_async_remote_copy(
            src_ref=lower.at[p, pl.ds(0, HB)],
            dst_ref=heads.at[p, pl.ds((n - off - 1) * HB, HB)],
            send_sem=head_send.at[off - 1],
            recv_sem=head_recv.at[p, n - off - 1],
            device_id={"rows": lax.rem(me + off, n)},
            device_id_type=pl.DeviceIdType.MESH,
        )

    def term_copy(p, off):
        return pltpu.make_async_remote_copy(
            src_ref=send_terms.at[pl.ds((off - 1) * HB, HB)],
            dst_ref=terms.at[p, pl.ds((n - off - 1) * HB, HB)],
            send_sem=term_send.at[off - 1],
            recv_sem=term_recv.at[p, n - off - 1],
            device_id={"rows": lax.rem(me + off, n)},
            device_id_type=pl.DeviceIdType.MESH,
        )

    def dot(a, b):
        return jnp.dot(a, b, preferred_element_type=F32)

    def sweep(s, last):
        p = lax.rem(s, 2)
        q = 1 - p
        for off in range(1, n):
            head_copy(p, off).start()

        zero = jnp.zeros(upper.shape[2:], F32)

        def running(first, pairs, blocks_of, weights, sums):
            step = pick_unroll(pairs, 24)
            group = pick_unroll(step, 8)

            def go(i, acc):
                for g in range(step // group):
                    found = []
                    for u in range(group):
                        j = i * step + g * group + u
                        lhs, rhs = [], []
                        for side in range(2):
                            e = meta[2 * (first + j) + side]
                            k, c = split(e, blocks_of)
                            lhs.append(upper[p, k])
                            rhs.append(weights[k, c])
                        found.append(dot(jnp.concatenate(lhs, 1), jnp.concatenate(rhs, 0)))
                    for u in range(group):
                        j = i * step + g * group + u
                        acc = acc * meta[at_keep + first + j].astype(F32) + found[u]
                        sums[j + 1] = acc.astype(sums.dtype)
                return acc

            lax.fori_loop(0, pairs // step, go, zero)

        running(0, far_pairs, far, far_w, far_sum)
        for off in range(1, n):
            for h in range(HB):
                row = (off - 1) * HB + h
                send_terms[row] = far_sum[meta[at_far_last + row]]
            term_copy(p, off).start()
        running(far_pairs, near_pairs, NEAR, near_w, near_sum)

        def bottom(k, extra):
            value = driven(k, 1) + near_sum[meta[at_near_last + k]]
            for row in range(extra):
                value = value + terms[p, row * HB + k].astype(F32)
            value = rotated(value)
            if last:
                out_l[k] = value
            else:
                lower[q, k] = value.astype(BF16)

        def bottom_step(k, carry):
            bottom(k, 0)
            return carry

        lax.fori_loop(HB, slots, bottom_step, 0, unroll=4)

        for off in range(1, n):
            head_copy(p, off).wait_recv()
        for row in range(far_rows):
            far_heads[row] = heads[p, row]

        step_top = pick_unroll(slots, 8)
        group_top = pick_unroll(step_top, 4)

        def top_step(i, carry):
            for g in range(step_top // group_top):
                found = []
                for u in range(group_top):
                    k = i * step_top + g * group_top + u
                    tiles = [lower[p, k]]
                    for c in range(NEAR - 1):
                        tiles.append(lower[p, meta[at_near_col + k * (NEAR - 1) + c]])
                    for c in range(far):
                        tiles.append(far_heads[meta[at_far_col + k * far + c]])
                    found.append(dot(jnp.concatenate(tiles, 1), turned[k]))
                for u in range(group_top):
                    k = i * step_top + g * group_top + u
                    alive = (k < meta[at_count]).astype(F32)
                    value = rotated(driven(k, 0) + found[u] * alive)
                    if last:
                        out_u[k] = value
                    else:
                        upper[q, k] = value.astype(BF16)
            return carry

        lax.fori_loop(0, slots // step_top, top_step, 0)
        if last:
            write_u.start()

        for off in range(1, n):
            term_copy(p, off).wait_recv()
        for k in range(HB):
            bottom(k, n - 1)
        if last:
            write_l.start()
        for off in range(1, n):
            head_copy(p, off).wait_send()
            term_copy(p, off).wait_send()

    write_u = pltpu.make_async_copy(out_u, out.at[:, 0], out_sem.at[0])
    write_l = pltpu.make_async_copy(out_l, out.at[:, 1], out_sem.at[1])

    def turn(i, carry):
        load_far(i).wait()
        load_near(i).wait()
        for u in range(chunk):
            k = i * chunk + u
            for c in range(NEAR + far):
                block = near_w[k, c] if c < NEAR else far_w[k, c - NEAR]
                turned[k, c * width:(c + 1) * width] = block.T
        return carry

    lax.fori_loop(0, slots // chunk, turn, 0)

    def middle(s, carry):
        sweep(s, False)
        return carry

    lax.fori_loop(0, ITERS - 1, middle, 0)
    sweep(ITERS - 1, True)
    write_u.wait()
    write_l.wait()


def plan(columns, counts, me, n):
    slots, stored = columns.shape
    far = stored - NEAR
    owner = columns // slots
    within = columns - owner * slots
    rel = lax.rem(owner - me + n, n)
    far_rows = (n - 1) * HB
    far_pairs, near_pairs = pair_counts(slots, far, n)
    near_all = within[:, :NEAR].reshape(-1)
    far_col = jnp.clip((rel - 1) * HB + within, 0, far_rows - 1)[:, NEAR:].reshape(-1)
    far_total = far_col.shape[0]
    dest = jnp.concatenate([far_col, far_rows + near_all])
    here = jnp.arange(dest.shape[0], dtype=jnp.int32)
    entry = jnp.where(here < far_total, here, here - far_total)
    rows = jnp.arange(far_rows + slots, dtype=jnp.int32)
    same = dest[None, :] == dest[:, None]
    order = jnp.sum((same & (here[None, :] < here[:, None])).astype(jnp.int32), 1)
    even = 1 - (order & 1)
    is_near = (rows >= far_rows).astype(jnp.int32)
    dest_near = (dest >= far_rows).astype(jnp.int32)
    ahead_rows = is_near * far_pairs + jnp.sum(
        jnp.where((dest[None, :] < rows[:, None]) & (dest_near[None, :] == is_near[:, None]),
                  even[None, :], 0), 1)
    own_rows = jnp.sum(jnp.where(dest[None, :] == rows[:, None], even[None, :], 0), 1)
    ahead = dest_near * far_pairs + jnp.sum(
        jnp.where((dest[None, :] < dest[:, None]) & (dest_near[None, :] == dest_near[:, None]),
                  even[None, :], 0), 1)
    place = 2 * ahead + order
    pairs = far_pairs + near_pairs
    spots = jnp.arange(2 * pairs, dtype=jnp.int32)
    empty = jnp.where(spots < 2 * far_pairs, slots * far, slots * NEAR)
    listed = jnp.sum(
        jnp.where(place[None, :] == spots[:, None], entry[None, :] - empty[:, None], 0), 1
    ) + empty
    pair_ids = jnp.arange(pairs, dtype=jnp.int32)
    starts = (ahead_rows[None, :] == pair_ids[:, None]) & (own_rows[None, :] > 0)
    keep = 1 - jnp.sum(starts.astype(jnp.int32), 1)
    ends = jnp.where(own_rows > 0, ahead_rows + own_rows - is_near * far_pairs, 0)
    return jnp.concatenate(
        [listed, keep, ends, within[:, 1:NEAR].reshape(-1), far_col, counts]
    )


def body(blocks, columns, counts, start_block, shift_radius, shift_angle):
    me = lax.axis_index("rows")
    n = lax.axis_size("rows")
    slots, stored, width = blocks.shape[0], blocks.shape[1], blocks.shape[-1]
    far = stored - NEAR
    shifts = shift_radius.shape[0]
    two_nvec = start_block.shape[2]
    cols = shifts * two_nvec
    meta = plan(columns, counts, me, n)
    weight = jnp.concatenate(
        [jnp.cos(shift_angle) / shift_radius, -jnp.sin(shift_angle) / shift_radius]
    )
    far_rows = (n - 1) * HB
    far_pairs, near_pairs = pair_counts(slots, far, n)
    flops = ITERS * 4 * slots * stored * width * width * cols
    smem = pl.BlockSpec(memory_space=pltpu.SMEM)
    hbm = pl.BlockSpec(memory_space=pl.ANY)
    return pl.pallas_call(
        functools.partial(kernel, n, slots, far, two_nvec // 2, shifts),
        out_shape=jax.ShapeDtypeStruct((slots, 2, cols, width), F32),
        in_specs=[smem, smem, hbm, hbm],
        out_specs=hbm,
        scratch_shapes=[
            pltpu.VMEM((slots + 1, NEAR, width, width), BF16),
            pltpu.VMEM((slots + 1, far, width, width), BF16),
            pltpu.VMEM((slots, stored * width, width), BF16),
            pltpu.VMEM(start_block.shape, F32),
            pltpu.VMEM((2, slots + 1, cols, width), BF16),
            pltpu.VMEM((2, slots, cols, width), BF16),
            pltpu.VMEM((near_pairs + 1, cols, width), F32),
            pltpu.VMEM((far_pairs + 1, cols, width), BF16),
            pltpu.VMEM((far_rows, cols, width), BF16),
            pltpu.VMEM((2, far_rows, cols, width), BF16),
            pltpu.VMEM((far_rows, cols, width), BF16),
            pltpu.VMEM((2, far_rows, cols, width), BF16),
            pltpu.VMEM((slots, cols, width), F32),
            pltpu.VMEM((slots, cols, width), F32),
            pltpu.SemaphoreType.DMA((1,)),
            pltpu.SemaphoreType.DMA((slots // pick_unroll(slots, 8),)),
            pltpu.SemaphoreType.DMA((slots // pick_unroll(slots, 8),)),
            pltpu.SemaphoreType.DMA((2,)),
            pltpu.SemaphoreType.DMA((n - 1,)),
            pltpu.SemaphoreType.DMA((2, n - 1)),
            pltpu.SemaphoreType.DMA((n - 1,)),
            pltpu.SemaphoreType.DMA((2, n - 1)),
        ],
        compiler_params=pltpu.CompilerParams(
            collective_id=0, has_side_effects=True, vmem_limit_bytes=56 * 1024 * 1024
        ),
        cost_estimate=pl.CostEstimate(
            flops=flops, bytes_accessed=2 * blocks.size, transcendentals=0
        ),
    )(meta, weight, blocks, start_block)


def solution(mesh):
    placed = (
        P("rows", None, None, None),
        P("rows", None),
        P("rows"),
        P("rows", None, None, None),
        P("dom"),
        P("dom"),
    )
    return jax.shard_map(
        body,
        mesh=mesh,
        in_specs=placed,
        out_specs=P(("dom", "rows"), None, None, None),
        check_vma=False,
    )
```

```python
import functools

import jax
import jax.numpy as jnp
from jax import lax
from jax.experimental import pallas as pl
from jax.experimental.pallas import tpu as pltpu
from jax.sharding import PartitionSpec as P

HB = 2
ITERS = 4
NEAR = 4
F32 = jnp.float32
BF16 = jnp.bfloat16


def pick_unroll(total, want):
    while total % want:
        want -= 1
    return want


def pair_counts(slots, far, n):
    far_rows = (n - 1) * HB
    far_pairs = (slots * far + far_rows) // 2
    near_pairs = (slots * NEAR + slots) // 2
    return -(-far_pairs // 8) * 8, -(-near_pairs // 8) * 8


def split(entry, width):
    if width & (width - 1):
        k = lax.div(entry, jnp.int32(width))
        return k, entry - k * width
    shift = width.bit_length() - 1
    return lax.shift_right_logical(entry, jnp.int32(shift)), entry & (width - 1)


def kernel(
    n, slots, far, nvec, shifts,
    meta, weight, blocks, start, out,
    near_w, far_w, turned, drive, upper, lower, near_sum, far_sum,
    pair_out, pair_in, send_terms, heads, far_heads, terms, out_u, out_l,
    load_sem, far_sem, near_sem, out_sem, head_send, head_recv, pass_send, pass_recv,
    pair_send, pair_recv, term_send, term_recv,
):
    me = lax.axis_index("rows")
    near_total = slots * (NEAR - 1)
    far_total = slots * far
    far_rows = (n - 1) * HB
    far_pairs, near_pairs = pair_counts(slots, far, n)
    chips = n // 2
    core = lax.rem(me, 2)
    chip = me // 2

    def partner(off):
        if off == 0:
            return chip * 2 + 1 - core
        return lax.rem(chip + off, chips) * 2 + core

    at_keep = 2 * (far_pairs + near_pairs)
    at_far_last = at_keep + far_pairs + near_pairs
    at_near_last = at_far_last + far_rows
    at_near_col = at_near_last + slots
    at_far_col = at_near_col + near_total
    at_count = at_far_col + far_total

    load_start = pltpu.make_async_copy(start, drive, load_sem.at[0])
    chunk = pick_unroll(slots, 8)
    width = turned.shape[2]

    def load_far(i):
        rows = pl.ds(i * chunk, chunk)
        return pltpu.make_async_copy(blocks.at[rows, NEAR:], far_w.at[rows], far_sem.at[i])

    def load_near(i):
        rows = pl.ds(i * chunk, chunk)
        return pltpu.make_async_copy(blocks.at[rows, :NEAR], near_w.at[rows], near_sem.at[i])

    load_start.start()
    for i in range(slots // chunk):
        load_far(i).start()
        load_near(i).start()

    barrier = pltpu.get_barrier_semaphore()
    for off in range(chips):
        pl.semaphore_signal(
            barrier, inc=1, device_id={"rows": partner(off)},
            device_id_type=pl.DeviceIdType.MESH,
        )

    def rotated(values):
        pieces = []
        for s in range(shifts):
            re = values[(2 * s) * nvec:(2 * s + 1) * nvec]
            im = values[(2 * s + 1) * nvec:(2 * s + 2) * nvec]
            w_re = weight[s]
            w_im = weight[shifts + s]
            pieces.append(w_re * re - w_im * im)
            pieces.append(w_re * im + w_im * re)
        return jnp.concatenate(pieces, 0)

    def driven(k, half):
        return jnp.concatenate([drive[k, half]] * shifts, 0)

    load_start.wait()

    def begin(k, carry):
        alive = (k < meta[at_count]).astype(F32)
        drive[k] = drive[k] * alive
        upper[0, k] = rotated(driven(k, 0)).astype(BF16)
        lower[0, k] = rotated(driven(k, 1)).astype(BF16)
        return carry

    lax.fori_loop(0, slots, begin, 0, unroll=2)
    for p in range(2):
        upper[p, slots] = jnp.zeros(upper.shape[2:], upper.dtype)
    near_w[slots, 0] = jnp.zeros(near_w.shape[2:], near_w.dtype)
    far_w[slots, 0] = jnp.zeros(far_w.shape[2:], far_w.dtype)
    near_sum[0] = jnp.zeros(near_sum.shape[1:], near_sum.dtype)
    far_sum[0] = jnp.zeros(far_sum.shape[1:], far_sum.dtype)
    pl.semaphore_wait(barrier, chips)

    def send(source, target, send_sem, recv_sem, off):
        return pltpu.make_async_remote_copy(
            src_ref=source, dst_ref=target, send_sem=send_sem, recv_sem=recv_sem,
            device_id={"rows": partner(off)}, device_id_type=pl.DeviceIdType.MESH,
        )

    def head_copy(p, off):
        there = 0 if off == 0 else 2 * (chips - off) - 1
        return send(
            lower.at[p, pl.ds(0, HB)], heads.at[p, pl.ds(there * HB, HB)],
            head_send.at[off], head_recv.at[p, 0 if off == 0 else chips - off], off,
        )

    def pass_copy(p, off):
        return send(
            heads.at[p, pl.ds((2 * off - 1) * HB, HB)], heads.at[p, pl.ds(2 * off * HB, HB)],
            pass_send.at[off - 1], pass_recv.at[p, off - 1], 0,
        )

    def pair_copy(p):
        return send(pair_out, pair_in.at[p], pair_send.at[0], pair_recv.at[p], 0)

    def term_copy(p, off):
        return send(
            send_terms.at[pl.ds((off - 1) * HB, HB)],
            terms.at[p, pl.ds((chips - off - 1) * HB, HB)],
            term_send.at[off - 1], term_recv.at[p, chips - off - 1], off,
        )

    def dot(a, b):
        return jnp.dot(a, b, preferred_element_type=F32)

    def sweep(s, last):
        p = lax.rem(s, 2)
        q = 1 - p
        for off in range(1, chips):
            head_copy(p, off).start()
        head_copy(p, 0).start()

        zero = jnp.zeros(upper.shape[2:], F32)

        def running(first, low, high, acc, blocks_of, weights, sums):
            step = pick_unroll(high - low, 24)
            group = pick_unroll(step, 8)

            def go(i, acc):
                for g in range(step // group):
                    found = []
                    for u in range(group):
                        j = low + i * step + g * group + u
                        lhs, rhs = [], []
                        for side in range(2):
                            e = meta[2 * (first + j) + side]
                            k, c = split(e, blocks_of)
                            lhs.append(upper[p, k])
                            rhs.append(weights[k, c])
                        found.append(dot(jnp.concatenate(lhs, 1), jnp.concatenate(rhs, 0)))
                    for u in range(group):
                        j = low + i * step + g * group + u
                        acc = acc * meta[at_keep + first + j].astype(F32) + found[u]
                        sums[j + 1] = acc.astype(sums.dtype)
                return acc

            return lax.fori_loop(0, (high - low) // step, go, acc)

        running(0, 0, far_pairs, zero, far, far_w, far_sum)
        for off in range(chips):
            for h in range(HB):
                row = 2 * off * HB + h
                pair_out[off * HB + h] = far_sum[meta[at_far_last + row]]
        pair_copy(p).start()
        half = near_pairs // 2
        acc = running(far_pairs, 0, half, zero, NEAR, near_w, near_sum)
        pair_copy(p).wait_recv()
        for off in range(1, chips):
            for h in range(HB):
                row = (2 * off - 1) * HB + h
                send_terms[(off - 1) * HB + h] = (
                    far_sum[meta[at_far_last + row]] + pair_in[p, off * HB + h]
                ).astype(BF16)
            term_copy(p, off).start()
        for off in range(1, chips):
            head_copy(p, chips - off).wait_recv()
            pass_copy(p, off).start()
        running(far_pairs, half, near_pairs, acc, NEAR, near_w, near_sum)

        def bottom(k, extra):
            value = driven(k, 1) + near_sum[meta[at_near_last + k]]
            if extra:
                value = value + pair_in[p, k]
                for off in range(chips - 1):
                    value = value + terms[p, off * HB + k].astype(F32)
            value = rotated(value)
            if last:
                out_l[k] = value
            else:
                lower[q, k] = value.astype(BF16)

        def bottom_step(k, carry):
            bottom(k, False)
            return carry

        lax.fori_loop(HB, slots, bottom_step, 0, unroll=4)

        head_copy(p, 0).wait_recv()
        for off in range(1, chips):
            pass_copy(p, off).wait_recv()
        for row in range(far_rows):
            far_heads[row] = heads[p, row]

        step_top = pick_unroll(slots, 8)
        group_top = pick_unroll(step_top, 4)

        def top_step(i, carry):
            for g in range(step_top // group_top):
                found = []
                for u in range(group_top):
                    k = i * step_top + g * group_top + u
                    tiles = [lower[p, k]]
                    for c in range(NEAR - 1):
                        tiles.append(lower[p, meta[at_near_col + k * (NEAR - 1) + c]])
                    for c in range(far):
                        tiles.append(far_heads[meta[at_far_col + k * far + c]])
                    found.append(dot(jnp.concatenate(tiles, 1), turned[k]))
                for u in range(group_top):
                    k = i * step_top + g * group_top + u
                    alive = (k < meta[at_count]).astype(F32)
                    value = rotated(driven(k, 0) + found[u] * alive)
                    if last:
                        out_u[k] = value
                    else:
                        upper[q, k] = value.astype(BF16)
            return carry

        lax.fori_loop(0, slots // step_top, top_step, 0)
        if last:
            write_u.start()

        for off in range(1, chips):
            term_copy(p, off).wait_recv()
        for k in range(HB):
            bottom(k, True)
        if last:
            write_l.start()
        pair_copy(p).wait_send()
        for off in range(chips):
            head_copy(p, off).wait_send()
        for off in range(1, chips):
            pass_copy(p, off).wait_send()
            term_copy(p, off).wait_send()

    write_u = pltpu.make_async_copy(out_u, out.at[:, 0], out_sem.at[0])
    write_l = pltpu.make_async_copy(out_l, out.at[:, 1], out_sem.at[1])

    def turn(i, carry):
        load_far(i).wait()
        load_near(i).wait()
        for u in range(chunk):
            k = i * chunk + u
            for c in range(NEAR + far):
                block = near_w[k, c] if c < NEAR else far_w[k, c - NEAR]
                turned[k, c * width:(c + 1) * width] = block.T
        return carry

    lax.fori_loop(0, slots // chunk, turn, 0)

    def middle(s, carry):
        sweep(s, False)
        return carry

    lax.fori_loop(0, ITERS - 1, middle, 0)
    sweep(ITERS - 1, True)
    write_u.wait()
    write_l.wait()


def plan(columns, counts, me, n):
    slots, stored = columns.shape
    far = stored - NEAR
    owner = columns // slots
    within = columns - owner * slots
    chips = n // 2
    rel = 2 * lax.rem(owner // 2 - me // 2 + chips, chips) + lax.rem(owner + me, 2)
    far_rows = (n - 1) * HB
    far_pairs, near_pairs = pair_counts(slots, far, n)
    near_all = within[:, :NEAR].reshape(-1)
    far_col = jnp.clip((rel - 1) * HB + within, 0, far_rows - 1)[:, NEAR:].reshape(-1)
    far_total = far_col.shape[0]
    dest = jnp.concatenate([far_col, far_rows + near_all])
    here = jnp.arange(dest.shape[0], dtype=jnp.int32)
    entry = jnp.where(here < far_total, here, here - far_total)
    rows = jnp.arange(far_rows + slots, dtype=jnp.int32)
    same = dest[None, :] == dest[:, None]
    order = jnp.sum((same & (here[None, :] < here[:, None])).astype(jnp.int32), 1)
    even = 1 - (order & 1)
    is_near = (rows >= far_rows).astype(jnp.int32)
    dest_near = (dest >= far_rows).astype(jnp.int32)
    ahead_rows = is_near * far_pairs + jnp.sum(
        jnp.where((dest[None, :] < rows[:, None]) & (dest_near[None, :] == is_near[:, None]),
                  even[None, :], 0), 1)
    own_rows = jnp.sum(jnp.where(dest[None, :] == rows[:, None], even[None, :], 0), 1)
    ahead = dest_near * far_pairs + jnp.sum(
        jnp.where((dest[None, :] < dest[:, None]) & (dest_near[None, :] == dest_near[:, None]),
                  even[None, :], 0), 1)
    place = 2 * ahead + order
    pairs = far_pairs + near_pairs
    spots = jnp.arange(2 * pairs, dtype=jnp.int32)
    empty = jnp.where(spots < 2 * far_pairs, slots * far, slots * NEAR)
    listed = jnp.sum(
        jnp.where(place[None, :] == spots[:, None], entry[None, :] - empty[:, None], 0), 1
    ) + empty
    pair_ids = jnp.arange(pairs, dtype=jnp.int32)
    starts = (ahead_rows[None, :] == pair_ids[:, None]) & (own_rows[None, :] > 0)
    keep = 1 - jnp.sum(starts.astype(jnp.int32), 1)
    ends = jnp.where(own_rows > 0, ahead_rows + own_rows - is_near * far_pairs, 0)
    return jnp.concatenate(
        [listed, keep, ends, within[:, 1:NEAR].reshape(-1), far_col, counts]
    )


def body(blocks, columns, counts, start_block, shift_radius, shift_angle):
    me = lax.axis_index("rows")
    n = lax.axis_size("rows")
    slots, stored, width = blocks.shape[0], blocks.shape[1], blocks.shape[-1]
    far = stored - NEAR
    shifts = shift_radius.shape[0]
    two_nvec = start_block.shape[2]
    cols = shifts * two_nvec
    meta = plan(columns, counts, me, n)
    weight = jnp.concatenate(
        [jnp.cos(shift_angle) / shift_radius, -jnp.sin(shift_angle) / shift_radius]
    )
    chips = n // 2
    far_rows = (n - 1) * HB
    far_pairs, near_pairs = pair_counts(slots, far, n)
    flops = ITERS * 4 * slots * stored * width * width * cols
    smem = pl.BlockSpec(memory_space=pltpu.SMEM)
    hbm = pl.BlockSpec(memory_space=pl.ANY)
    return pl.pallas_call(
        functools.partial(kernel, n, slots, far, two_nvec // 2, shifts),
        out_shape=jax.ShapeDtypeStruct((slots, 2, cols, width), F32),
        in_specs=[smem, smem, hbm, hbm],
        out_specs=hbm,
        scratch_shapes=[
            pltpu.VMEM((slots + 1, NEAR, width, width), BF16),
            pltpu.VMEM((slots + 1, far, width, width), BF16),
            pltpu.VMEM((slots, stored * width, width), BF16),
            pltpu.VMEM(start_block.shape, F32),
            pltpu.VMEM((2, slots + 1, cols, width), BF16),
            pltpu.VMEM((2, slots, cols, width), BF16),
            pltpu.VMEM((near_pairs + 1, cols, width), F32),
            pltpu.VMEM((far_pairs + 1, cols, width), F32),
            pltpu.VMEM((chips * HB, cols, width), F32),
            pltpu.VMEM((2, chips * HB, cols, width), F32),
            pltpu.VMEM(((chips - 1) * HB, cols, width), BF16),
            pltpu.VMEM((2, far_rows, cols, width), BF16),
            pltpu.VMEM((far_rows, cols, width), BF16),
            pltpu.VMEM((2, (chips - 1) * HB, cols, width), BF16),
            pltpu.VMEM((slots, cols, width), F32),
            pltpu.VMEM((slots, cols, width), F32),
            pltpu.SemaphoreType.DMA((1,)),
            pltpu.SemaphoreType.DMA((slots // pick_unroll(slots, 8),)),
            pltpu.SemaphoreType.DMA((slots // pick_unroll(slots, 8),)),
            pltpu.SemaphoreType.DMA((2,)),
            pltpu.SemaphoreType.DMA((chips,)),
            pltpu.SemaphoreType.DMA((2, chips)),
            pltpu.SemaphoreType.DMA((chips - 1,)),
            pltpu.SemaphoreType.DMA((2, chips - 1)),
            pltpu.SemaphoreType.DMA((1,)),
            pltpu.SemaphoreType.DMA((2,)),
            pltpu.SemaphoreType.DMA((chips - 1,)),
            pltpu.SemaphoreType.DMA((2, chips - 1)),
        ],
        compiler_params=pltpu.CompilerParams(
            collective_id=0, has_side_effects=True, vmem_limit_bytes=56 * 1024 * 1024
        ),
        cost_estimate=pl.CostEstimate(
            flops=flops, bytes_accessed=2 * blocks.size, transcendentals=0
        ),
    )(meta, weight, blocks, start_block)


def solution(mesh):
    placed = (
        P("rows", None, None, None),
        P("rows", None),
        P("rows"),
        P("rows", None, None, None),
        P("dom"),
        P("dom"),
    )
    return jax.shard_map(
        body,
        mesh=mesh,
        in_specs=placed,
        out_specs=P(("dom", "rows"), None, None, None),
        check_vma=False,
    )
```

```python
import functools

import jax
import jax.numpy as jnp
from jax import lax
from jax.experimental import pallas as pl
from jax.experimental.pallas import tpu as pltpu
from jax.sharding import PartitionSpec as P

HB = 2
ITERS = 4
NEAR = 4
F32 = jnp.float32
BF16 = jnp.bfloat16


def pick_unroll(total, want):
    while total % want:
        want -= 1
    return want


def pair_counts(slots, far, n):
    far_rows = (n - 1) * HB
    far_pairs = (slots * far + far_rows) // 2
    near_pairs = (slots * NEAR + slots) // 2
    return -(-far_pairs // 8) * 8, -(-near_pairs // 8) * 8


def split(entry, width):
    if width & (width - 1):
        k = lax.div(entry, jnp.int32(width))
        return k, entry - k * width
    shift = width.bit_length() - 1
    return lax.shift_right_logical(entry, jnp.int32(shift)), entry & (width - 1)


def kernel(
    n, slots, far, nvec, shifts,
    meta, weight, blocks, start, out,
    near_w, far_w, turned, drive, upper, lower, near_sum, far_sum,
    pair_out, pair_in, send_terms, heads, far_heads, terms, out_u, out_l,
    load_sem, far_sem, near_sem, out_sem, head_send, head_recv, pass_send, pass_recv,
    pair_send, pair_recv, term_send, term_recv,
):
    me = lax.axis_index("rows")
    near_total = slots * (NEAR - 1)
    far_total = slots * far
    far_rows = (n - 1) * HB
    far_pairs, near_pairs = pair_counts(slots, far, n)
    chips = n // 2
    core = lax.rem(me, 2)
    chip = me // 2

    def partner(off):
        if off == 0:
            return chip * 2 + 1 - core
        return lax.rem(chip + off, chips) * 2 + core

    at_keep = 2 * (far_pairs + near_pairs)
    at_far_last = at_keep + far_pairs + near_pairs
    at_near_last = at_far_last + far_rows
    at_near_col = at_near_last + slots
    at_far_col = at_near_col + near_total
    at_count = at_far_col + far_total

    load_start = pltpu.make_async_copy(start, drive, load_sem.at[0])
    chunk = pick_unroll(slots, 8)
    width = turned.shape[2]

    def load_far(i):
        rows = pl.ds(i * chunk, chunk)
        return pltpu.make_async_copy(blocks.at[rows, NEAR:], far_w.at[rows], far_sem.at[i])

    def load_near(i):
        rows = pl.ds(i * chunk, chunk)
        return pltpu.make_async_copy(blocks.at[rows, :NEAR], near_w.at[rows], near_sem.at[i])

    load_start.start()
    for i in range(slots // chunk):
        load_far(i).start()
        load_near(i).start()

    barrier = pltpu.get_barrier_semaphore()
    for off in range(chips):
        pl.semaphore_signal(
            barrier, inc=1, device_id={"rows": partner(off)},
            device_id_type=pl.DeviceIdType.MESH,
        )

    def rotated(values):
        pieces = []
        for s in range(shifts):
            re = values[(2 * s) * nvec:(2 * s + 1) * nvec]
            im = values[(2 * s + 1) * nvec:(2 * s + 2) * nvec]
            w_re = weight[s]
            w_im = weight[shifts + s]
            pieces.append(w_re * re - w_im * im)
            pieces.append(w_re * im + w_im * re)
        return jnp.concatenate(pieces, 0)

    def driven(k, half):
        return jnp.concatenate([drive[k, half]] * shifts, 0)

    load_start.wait()

    def begin(k, carry):
        alive = (k < meta[at_count]).astype(F32)
        drive[k] = drive[k] * alive
        upper[0, k] = rotated(driven(k, 0)).astype(BF16)
        lower[0, k] = rotated(driven(k, 1)).astype(BF16)
        return carry

    lax.fori_loop(0, slots, begin, 0, unroll=2)
    for p in range(2):
        upper[p, slots] = jnp.zeros(upper.shape[2:], upper.dtype)
    near_w[slots, 0] = jnp.zeros(near_w.shape[2:], near_w.dtype)
    far_w[slots, 0] = jnp.zeros(far_w.shape[2:], far_w.dtype)
    near_sum[0] = jnp.zeros(near_sum.shape[1:], near_sum.dtype)
    far_sum[0] = jnp.zeros(far_sum.shape[1:], far_sum.dtype)
    pl.semaphore_wait(barrier, chips)

    def send(source, target, send_sem, recv_sem, off):
        return pltpu.make_async_remote_copy(
            src_ref=source, dst_ref=target, send_sem=send_sem, recv_sem=recv_sem,
            device_id={"rows": partner(off)}, device_id_type=pl.DeviceIdType.MESH,
        )

    def head_copy(p, off):
        there = 0 if off == 0 else 2 * (chips - off) - 1
        return send(
            lower.at[p, pl.ds(0, HB)], heads.at[p, pl.ds(there * HB, HB)],
            head_send.at[off], head_recv.at[p, 0 if off == 0 else chips - off], off,
        )

    def pass_copy(p, off):
        return send(
            heads.at[p, pl.ds((2 * off - 1) * HB, HB)], heads.at[p, pl.ds(2 * off * HB, HB)],
            pass_send.at[off - 1], pass_recv.at[p, off - 1], 0,
        )

    def pair_copy(p):
        return send(pair_out, pair_in.at[p], pair_send.at[0], pair_recv.at[p], 0)

    def term_copy(p, off):
        return send(
            send_terms.at[pl.ds((off - 1) * HB, HB)],
            terms.at[p, pl.ds((chips - off - 1) * HB, HB)],
            term_send.at[off - 1], term_recv.at[p, chips - off - 1], off,
        )

    def dot(a, b):
        return jnp.dot(a, b, preferred_element_type=F32)

    def two_by_two(left, right):
        found = []
        for i in range(0, len(left) - 1, 2):
            rows, cols = left[i].shape[0], right[i].shape[1]
            both = dot(jnp.concatenate(left[i:i + 2], 0), jnp.concatenate(right[i:i + 2], 1))
            found += [both[:rows, :cols], both[rows:, cols:]]
        if len(left) % 2:
            found.append(dot(left[-1], right[-1]))
        return found

    def sweep(s, last):
        p = lax.rem(s, 2)
        q = 1 - p
        for off in range(1, chips):
            head_copy(p, off).start()
        head_copy(p, 0).start()

        zero = jnp.zeros(upper.shape[2:], F32)

        def running(first, low, high, acc, blocks_of, weights, sums):
            step = pick_unroll(high - low, 16)
            group = pick_unroll(step, 8)

            def go(i, acc):
                for g in range(step // group):
                    left, right = [], []
                    for u in range(group):
                        j = low + i * step + g * group + u
                        lhs, rhs = [], []
                        for side in range(2):
                            e = meta[2 * (first + j) + side]
                            k, c = split(e, blocks_of)
                            lhs.append(upper[p, k])
                            rhs.append(weights[k, c])
                        left.append(jnp.concatenate(lhs, 1))
                        right.append(jnp.concatenate(rhs, 0))
                    found = two_by_two(left, right)
                    for u in range(group):
                        j = low + i * step + g * group + u
                        acc = acc * meta[at_keep + first + j].astype(F32) + found[u]
                        sums[j + 1] = acc.astype(sums.dtype)
                return acc

            return lax.fori_loop(0, (high - low) // step, go, acc)

        running(0, 0, far_pairs, zero, far, far_w, far_sum)
        for off in range(chips):
            for h in range(HB):
                row = 2 * off * HB + h
                pair_out[off * HB + h] = far_sum[meta[at_far_last + row]]
        pair_copy(p).start()
        half = near_pairs // 2
        acc = running(far_pairs, 0, half, zero, NEAR, near_w, near_sum)
        pair_copy(p).wait_recv()
        for off in range(1, chips):
            for h in range(HB):
                row = (2 * off - 1) * HB + h
                send_terms[(off - 1) * HB + h] = (
                    far_sum[meta[at_far_last + row]] + pair_in[p, off * HB + h]
                ).astype(BF16)
            term_copy(p, off).start()
        for off in range(1, chips):
            head_copy(p, chips - off).wait_recv()
            pass_copy(p, off).start()
        running(far_pairs, half, near_pairs, acc, NEAR, near_w, near_sum)

        def bottom(k, extra):
            value = driven(k, 1) + near_sum[meta[at_near_last + k]]
            if extra:
                value = value + pair_in[p, k]
                for off in range(chips - 1):
                    value = value + terms[p, off * HB + k].astype(F32)
            value = rotated(value)
            if last:
                out_l[k] = value
            else:
                lower[q, k] = value.astype(BF16)

        def bottom_step(k, carry):
            bottom(k, False)
            return carry

        lax.fori_loop(HB, slots, bottom_step, 0, unroll=4)

        head_copy(p, 0).wait_recv()
        for off in range(1, chips):
            pass_copy(p, off).wait_recv()
        for row in range(far_rows):
            far_heads[row] = heads[p, row]

        step_top = pick_unroll(slots, 8)
        group_top = pick_unroll(step_top, 4)

        def top_step(i, carry):
            for g in range(step_top // group_top):
                left, right = [], []
                for u in range(group_top):
                    k = i * step_top + g * group_top + u
                    tiles = [lower[p, k]]
                    for c in range(NEAR - 1):
                        tiles.append(lower[p, meta[at_near_col + k * (NEAR - 1) + c]])
                    for c in range(far):
                        tiles.append(far_heads[meta[at_far_col + k * far + c]])
                    left.append(jnp.concatenate(tiles, 1))
                    right.append(turned[k])
                found = two_by_two(left, right)
                for u in range(group_top):
                    k = i * step_top + g * group_top + u
                    alive = (k < meta[at_count]).astype(F32)
                    value = rotated(driven(k, 0) + found[u] * alive)
                    if last:
                        out_u[k] = value
                    else:
                        upper[q, k] = value.astype(BF16)
            return carry

        lax.fori_loop(0, slots // step_top, top_step, 0)
        if last:
            write_u.start()

        for off in range(1, chips):
            term_copy(p, off).wait_recv()
        for k in range(HB):
            bottom(k, True)
        if last:
            write_l.start()
        pair_copy(p).wait_send()
        for off in range(chips):
            head_copy(p, off).wait_send()
        for off in range(1, chips):
            pass_copy(p, off).wait_send()
            term_copy(p, off).wait_send()

    write_u = pltpu.make_async_copy(out_u, out.at[:, 0], out_sem.at[0])
    write_l = pltpu.make_async_copy(out_l, out.at[:, 1], out_sem.at[1])

    def turn(i, carry):
        load_far(i).wait()
        load_near(i).wait()
        for u in range(chunk):
            k = i * chunk + u
            for c in range(NEAR + far):
                block = near_w[k, c] if c < NEAR else far_w[k, c - NEAR]
                turned[k, c * width:(c + 1) * width] = block.T
        return carry

    lax.fori_loop(0, slots // chunk, turn, 0)

    def middle(s, carry):
        sweep(s, False)
        return carry

    lax.fori_loop(0, ITERS - 1, middle, 0)
    sweep(ITERS - 1, True)
    write_u.wait()
    write_l.wait()


def plan(columns, counts, me, n):
    slots, stored = columns.shape
    far = stored - NEAR
    owner = columns // slots
    within = columns - owner * slots
    chips = n // 2
    rel = 2 * lax.rem(owner // 2 - me // 2 + chips, chips) + lax.rem(owner + me, 2)
    far_rows = (n - 1) * HB
    far_pairs, near_pairs = pair_counts(slots, far, n)
    near_all = within[:, :NEAR].reshape(-1)
    far_col = jnp.clip((rel - 1) * HB + within, 0, far_rows - 1)[:, NEAR:].reshape(-1)
    far_total = far_col.shape[0]
    dest = jnp.concatenate([far_col, far_rows + near_all])
    here = jnp.arange(dest.shape[0], dtype=jnp.int32)
    entry = jnp.where(here < far_total, here, here - far_total)
    rows = jnp.arange(far_rows + slots, dtype=jnp.int32)
    same = dest[None, :] == dest[:, None]
    order = jnp.sum((same & (here[None, :] < here[:, None])).astype(jnp.int32), 1)
    even = 1 - (order & 1)
    is_near = (rows >= far_rows).astype(jnp.int32)
    dest_near = (dest >= far_rows).astype(jnp.int32)
    ahead_rows = is_near * far_pairs + jnp.sum(
        jnp.where((dest[None, :] < rows[:, None]) & (dest_near[None, :] == is_near[:, None]),
                  even[None, :], 0), 1)
    own_rows = jnp.sum(jnp.where(dest[None, :] == rows[:, None], even[None, :], 0), 1)
    ahead = dest_near * far_pairs + jnp.sum(
        jnp.where((dest[None, :] < dest[:, None]) & (dest_near[None, :] == dest_near[:, None]),
                  even[None, :], 0), 1)
    place = 2 * ahead + order
    pairs = far_pairs + near_pairs
    spots = jnp.arange(2 * pairs, dtype=jnp.int32)
    empty = jnp.where(spots < 2 * far_pairs, slots * far, slots * NEAR)
    listed = jnp.sum(
        jnp.where(place[None, :] == spots[:, None], entry[None, :] - empty[:, None], 0), 1
    ) + empty
    pair_ids = jnp.arange(pairs, dtype=jnp.int32)
    starts = (ahead_rows[None, :] == pair_ids[:, None]) & (own_rows[None, :] > 0)
    keep = 1 - jnp.sum(starts.astype(jnp.int32), 1)
    ends = jnp.where(own_rows > 0, ahead_rows + own_rows - is_near * far_pairs, 0)
    return jnp.concatenate(
        [listed, keep, ends, within[:, 1:NEAR].reshape(-1), far_col, counts]
    )


def body(blocks, columns, counts, start_block, shift_radius, shift_angle):
    me = lax.axis_index("rows")
    n = lax.axis_size("rows")
    slots, stored, width = blocks.shape[0], blocks.shape[1], blocks.shape[-1]
    far = stored - NEAR
    shifts = shift_radius.shape[0]
    two_nvec = start_block.shape[2]
    cols = shifts * two_nvec
    meta = plan(columns, counts, me, n)
    weight = jnp.concatenate(
        [jnp.cos(shift_angle) / shift_radius, -jnp.sin(shift_angle) / shift_radius]
    )
    chips = n // 2
    far_rows = (n - 1) * HB
    far_pairs, near_pairs = pair_counts(slots, far, n)
    flops = ITERS * 4 * slots * stored * width * width * cols
    smem = pl.BlockSpec(memory_space=pltpu.SMEM)
    hbm = pl.BlockSpec(memory_space=pl.ANY)
    return pl.pallas_call(
        functools.partial(kernel, n, slots, far, two_nvec // 2, shifts),
        out_shape=jax.ShapeDtypeStruct((slots, 2, cols, width), F32),
        in_specs=[smem, smem, hbm, hbm],
        out_specs=hbm,
        scratch_shapes=[
            pltpu.VMEM((slots + 1, NEAR, width, width), BF16),
            pltpu.VMEM((slots + 1, far, width, width), BF16),
            pltpu.VMEM((slots, stored * width, width), BF16),
            pltpu.VMEM(start_block.shape, F32),
            pltpu.VMEM((2, slots + 1, cols, width), BF16),
            pltpu.VMEM((2, slots, cols, width), BF16),
            pltpu.VMEM((near_pairs + 1, cols, width), F32),
            pltpu.VMEM((far_pairs + 1, cols, width), F32),
            pltpu.VMEM((chips * HB, cols, width), F32),
            pltpu.VMEM((2, chips * HB, cols, width), F32),
            pltpu.VMEM(((chips - 1) * HB, cols, width), BF16),
            pltpu.VMEM((2, far_rows, cols, width), BF16),
            pltpu.VMEM((far_rows, cols, width), BF16),
            pltpu.VMEM((2, (chips - 1) * HB, cols, width), BF16),
            pltpu.VMEM((slots, cols, width), F32),
            pltpu.VMEM((slots, cols, width), F32),
            pltpu.SemaphoreType.DMA((1,)),
            pltpu.SemaphoreType.DMA((slots // pick_unroll(slots, 8),)),
            pltpu.SemaphoreType.DMA((slots // pick_unroll(slots, 8),)),
            pltpu.SemaphoreType.DMA((2,)),
            pltpu.SemaphoreType.DMA((chips,)),
            pltpu.SemaphoreType.DMA((2, chips)),
            pltpu.SemaphoreType.DMA((chips - 1,)),
            pltpu.SemaphoreType.DMA((2, chips - 1)),
            pltpu.SemaphoreType.DMA((1,)),
            pltpu.SemaphoreType.DMA((2,)),
            pltpu.SemaphoreType.DMA((chips - 1,)),
            pltpu.SemaphoreType.DMA((2, chips - 1)),
        ],
        compiler_params=pltpu.CompilerParams(
            collective_id=0, has_side_effects=True, vmem_limit_bytes=56 * 1024 * 1024
        ),
        cost_estimate=pl.CostEstimate(
            flops=flops, bytes_accessed=2 * blocks.size, transcendentals=0
        ),
    )(meta, weight, blocks, start_block)


def solution(mesh):
    placed = (
        P("rows", None, None, None),
        P("rows", None),
        P("rows"),
        P("rows", None, None, None),
        P("dom"),
        P("dom"),
    )
    return jax.shard_map(
        body,
        mesh=mesh,
        in_specs=placed,
        out_specs=P(("dom", "rows"), None, None, None),
        check_vma=False,
    )
```

```python
import functools

import jax
import jax.numpy as jnp
from jax import lax
from jax.experimental import pallas as pl
from jax.experimental.pallas import tpu as pltpu
from jax.sharding import PartitionSpec as P

HB = 2
ITERS = 4
NEAR = 4
F32 = jnp.float32
BF16 = jnp.bfloat16


def pick_unroll(total, want):
    while total % want:
        want -= 1
    return want


def pair_counts(slots, far, n):
    far_rows = (n - 1) * HB
    far_pairs = (slots * far + far_rows) // 2
    near_pairs = (slots * NEAR + slots) // 2
    return -(-far_pairs // 8) * 8, -(-near_pairs // 8) * 8


def split(entry, width):
    if width & (width - 1):
        k = lax.div(entry, jnp.int32(width))
        return k, entry - k * width
    shift = width.bit_length() - 1
    return lax.shift_right_logical(entry, jnp.int32(shift)), entry & (width - 1)


def kernel(
    n, slots, far, nvec, shifts,
    meta, radius, angle, blocks, start, out,
    near_w, far_w, turned, weight, drive, upper, lower, near_sum, far_sum,
    pair_out, pair_in, send_terms, heads, far_heads, terms,
    load_sem, far_sem, near_sem, head_send, head_recv, pass_send, pass_recv,
    pair_send, pair_recv, term_send, term_recv,
):
    me = lax.axis_index("rows")
    near_total = slots * (NEAR - 1)
    far_total = slots * far
    far_rows = (n - 1) * HB
    far_pairs, near_pairs = pair_counts(slots, far, n)
    chips = n // 2
    core = lax.rem(me, 2)
    chip = me // 2

    def partner(off):
        if off == 0:
            return chip * 2 + 1 - core
        return lax.rem(chip + off, chips) * 2 + core

    at_keep = 2 * (far_pairs + near_pairs)
    at_far_last = at_keep + far_pairs + near_pairs
    at_near_last = at_far_last + far_rows
    at_near_col = at_near_last + slots
    at_far_col = at_near_col + near_total
    at_count = at_far_col + far_total

    load_start = pltpu.make_async_copy(start, drive, load_sem.at[0])
    chunk = pick_unroll(slots, 8)
    width = turned.shape[2]

    def load_far(i):
        rows = pl.ds(i * chunk, chunk)
        return pltpu.make_async_copy(blocks.at[rows, NEAR:], far_w.at[rows], far_sem.at[i])

    def load_near(i):
        rows = pl.ds(i * chunk, chunk)
        return pltpu.make_async_copy(blocks.at[rows, :NEAR], near_w.at[rows], near_sem.at[i])

    load_start.start()
    for i in range(slots // chunk):
        load_far(i).start()
        load_near(i).start()

    barrier = pltpu.get_barrier_semaphore()
    for off in range(chips):
        pl.semaphore_signal(
            barrier, inc=1, device_id={"rows": partner(off)},
            device_id_type=pl.DeviceIdType.MESH,
        )

    def rotated(values):
        pieces = []
        for s in range(shifts):
            re = values[(2 * s) * nvec:(2 * s + 1) * nvec]
            im = values[(2 * s + 1) * nvec:(2 * s + 2) * nvec]
            w_re = weight[s]
            w_im = weight[shifts + s]
            pieces.append(w_re * re - w_im * im)
            pieces.append(w_re * im + w_im * re)
        return jnp.concatenate(pieces, 0)

    def driven(k, half):
        return jnp.concatenate([drive[k, half]] * shifts, 0)

    for s in range(shifts):
        turn_by = jnp.full(weight.shape[1:], angle[s], F32)
        size = jnp.full(weight.shape[1:], radius[s], F32)
        weight[s] = jnp.cos(turn_by) / size
        weight[shifts + s] = -jnp.sin(turn_by) / size
    load_start.wait()

    def begin(k, carry):
        alive = (k < meta[at_count]).astype(F32)
        drive[k] = drive[k] * alive
        upper[0, k] = rotated(driven(k, 0)).astype(BF16)
        lower[0, k] = rotated(driven(k, 1)).astype(BF16)
        return carry

    lax.fori_loop(0, slots, begin, 0, unroll=2)
    for p in range(2):
        upper[p, slots] = jnp.zeros(upper.shape[2:], upper.dtype)
    near_w[slots, 0] = jnp.zeros(near_w.shape[2:], near_w.dtype)
    far_w[slots, 0] = jnp.zeros(far_w.shape[2:], far_w.dtype)
    near_sum[0] = jnp.zeros(near_sum.shape[1:], near_sum.dtype)
    far_sum[0] = jnp.zeros(far_sum.shape[1:], far_sum.dtype)
    pl.semaphore_wait(barrier, chips)

    def send(source, target, send_sem, recv_sem, off):
        return pltpu.make_async_remote_copy(
            src_ref=source, dst_ref=target, send_sem=send_sem, recv_sem=recv_sem,
            device_id={"rows": partner(off)}, device_id_type=pl.DeviceIdType.MESH,
        )

    def head_copy(p, off):
        there = 0 if off == 0 else 2 * (chips - off) - 1
        return send(
            lower.at[p, pl.ds(0, HB)], heads.at[p, pl.ds(there * HB, HB)],
            head_send.at[off], head_recv.at[p, 0 if off == 0 else chips - off], off,
        )

    def pass_copy(p, off):
        return send(
            heads.at[p, pl.ds((2 * off - 1) * HB, HB)], heads.at[p, pl.ds(2 * off * HB, HB)],
            pass_send.at[off - 1], pass_recv.at[p, off - 1], 0,
        )

    def pair_copy(p):
        return send(pair_out, pair_in.at[p], pair_send.at[0], pair_recv.at[p], 0)

    def term_copy(p, off):
        return send(
            send_terms.at[pl.ds((off - 1) * HB, HB)],
            terms.at[p, pl.ds((chips - off - 1) * HB, HB)],
            term_send.at[off - 1], term_recv.at[p, chips - off - 1], off,
        )

    def dot(a, b):
        return jnp.dot(a, b, preferred_element_type=F32)

    def sweep(s, last):
        p = lax.rem(s, 2)
        q = 1 - p
        for off in range(1, chips):
            head_copy(p, off).start()
        head_copy(p, 0).start()

        zero = jnp.zeros(upper.shape[2:], F32)

        def running(first, low, high, acc, blocks_of, weights, sums):
            step = pick_unroll(high - low, 40)
            group = pick_unroll(step, 8)

            def go(i, acc):
                for g in range(step // group):
                    found = []
                    for u in range(group):
                        j = low + i * step + g * group + u
                        lhs, rhs = [], []
                        for side in range(2):
                            e = meta[2 * (first + j) + side]
                            k, c = split(e, blocks_of)
                            lhs.append(upper[p, k])
                            rhs.append(weights[k, c])
                        found.append(dot(jnp.concatenate(lhs, 1), jnp.concatenate(rhs, 0)))
                    for u in range(group):
                        j = low + i * step + g * group + u
                        acc = acc * meta[at_keep + first + j].astype(F32) + found[u]
                        sums[j + 1] = acc.astype(sums.dtype)
                return acc

            return lax.fori_loop(0, (high - low) // step, go, acc)

        running(0, 0, far_pairs, zero, far, far_w, far_sum)
        for off in range(chips):
            for h in range(HB):
                row = 2 * off * HB + h
                pair_out[off * HB + h] = far_sum[meta[at_far_last + row]]
        pair_copy(p).start()
        half = near_pairs // 2
        acc = running(far_pairs, 0, half, zero, NEAR, near_w, near_sum)
        pair_copy(p).wait_recv()
        for off in range(1, chips):
            for h in range(HB):
                row = (2 * off - 1) * HB + h
                send_terms[(off - 1) * HB + h] = (
                    far_sum[meta[at_far_last + row]] + pair_in[p, off * HB + h]
                ).astype(BF16)
            term_copy(p, off).start()
        for off in range(1, chips):
            head_copy(p, chips - off).wait_recv()
            pass_copy(p, off).start()
        running(far_pairs, half, near_pairs, acc, NEAR, near_w, near_sum)

        def bottom(k, extra):
            value = driven(k, 1) + near_sum[meta[at_near_last + k]]
            if extra:
                value = value + pair_in[p, k]
                for off in range(chips - 1):
                    value = value + terms[p, off * HB + k].astype(F32)
            value = rotated(value)
            if last:
                out[k, 1] = value
            else:
                lower[q, k] = value.astype(BF16)

        def bottom_step(k, carry):
            bottom(k, False)
            return carry

        lax.fori_loop(HB, slots, bottom_step, 0, unroll=16)

        head_copy(p, 0).wait_recv()
        for off in range(1, chips):
            pass_copy(p, off).wait_recv()
        for row in range(far_rows):
            far_heads[row] = heads[p, row]

        step_top = pick_unroll(slots, 16)
        group_top = pick_unroll(step_top, 4)

        def top_step(i, carry):
            for g in range(step_top // group_top):
                found = []
                for u in range(group_top):
                    k = i * step_top + g * group_top + u
                    tiles = [lower[p, k]]
                    for c in range(NEAR - 1):
                        tiles.append(lower[p, meta[at_near_col + k * (NEAR - 1) + c]])
                    for c in range(far):
                        tiles.append(far_heads[meta[at_far_col + k * far + c]])
                    found.append(dot(jnp.concatenate(tiles, 1), turned[k]))
                for u in range(group_top):
                    k = i * step_top + g * group_top + u
                    alive = (k < meta[at_count]).astype(F32)
                    value = rotated(driven(k, 0) + found[u] * alive)
                    if last:
                        out[k, 0] = value
                    else:
                        upper[q, k] = value.astype(BF16)
            return carry

        lax.fori_loop(0, slots // step_top, top_step, 0)

        for off in range(1, chips):
            term_copy(p, off).wait_recv()
        for k in range(HB):
            bottom(k, True)
        pair_copy(p).wait_send()
        for off in range(chips):
            head_copy(p, off).wait_send()
        for off in range(1, chips):
            pass_copy(p, off).wait_send()
            term_copy(p, off).wait_send()


    def turn(i, carry):
        load_far(i).wait()
        load_near(i).wait()
        for u in range(chunk):
            k = i * chunk + u
            for c in range(NEAR + far):
                block = near_w[k, c] if c < NEAR else far_w[k, c - NEAR]
                turned[k, c * width:(c + 1) * width] = block.T
        return carry

    lax.fori_loop(0, slots // chunk, turn, 0)

    def middle(s, carry):
        sweep(s, False)
        return carry

    lax.fori_loop(0, ITERS - 1, middle, 0)
    sweep(ITERS - 1, True)


def plan(columns, counts, me, n):
    slots, stored = columns.shape
    far = stored - NEAR
    owner = columns // slots
    within = columns - owner * slots
    chips = n // 2
    rel = 2 * lax.rem(owner // 2 - me // 2 + chips, chips) + lax.rem(owner + me, 2)
    far_rows = (n - 1) * HB
    far_pairs, near_pairs = pair_counts(slots, far, n)
    near_all = within[:, :NEAR].reshape(-1)
    far_col = jnp.clip((rel - 1) * HB + within, 0, far_rows - 1)[:, NEAR:].reshape(-1)
    far_total = far_col.shape[0]
    dest = jnp.concatenate([far_col, far_rows + near_all])
    here = jnp.arange(dest.shape[0], dtype=jnp.int32)
    entry = jnp.where(here < far_total, here, here - far_total)
    rows = jnp.arange(far_rows + slots, dtype=jnp.int32)
    same = dest[None, :] == dest[:, None]
    order = jnp.sum((same & (here[None, :] < here[:, None])).astype(jnp.int32), 1)
    even = 1 - (order & 1)
    is_near = (rows >= far_rows).astype(jnp.int32)
    dest_near = (dest >= far_rows).astype(jnp.int32)
    ahead_rows = is_near * far_pairs + jnp.sum(
        jnp.where((dest[None, :] < rows[:, None]) & (dest_near[None, :] == is_near[:, None]),
                  even[None, :], 0), 1)
    own_rows = jnp.sum(jnp.where(dest[None, :] == rows[:, None], even[None, :], 0), 1)
    ahead = dest_near * far_pairs + jnp.sum(
        jnp.where((dest[None, :] < dest[:, None]) & (dest_near[None, :] == dest_near[:, None]),
                  even[None, :], 0), 1)
    place = 2 * ahead + order
    pairs = far_pairs + near_pairs
    spots = jnp.arange(2 * pairs, dtype=jnp.int32)
    empty = jnp.where(spots < 2 * far_pairs, slots * far, slots * NEAR)
    listed = jnp.sum(
        jnp.where(place[None, :] == spots[:, None], entry[None, :] - empty[:, None], 0), 1
    ) + empty
    pair_ids = jnp.arange(pairs, dtype=jnp.int32)
    starts = (ahead_rows[None, :] == pair_ids[:, None]) & (own_rows[None, :] > 0)
    keep = 1 - jnp.sum(starts.astype(jnp.int32), 1)
    ends = jnp.where(own_rows > 0, ahead_rows + own_rows - is_near * far_pairs, 0)
    return jnp.concatenate(
        [listed, keep, ends, within[:, 1:NEAR].reshape(-1), far_col, counts]
    )


def body(blocks, columns, counts, start_block, shift_radius, shift_angle):
    me = lax.axis_index("rows")
    n = lax.axis_size("rows")
    slots, stored, width = blocks.shape[0], blocks.shape[1], blocks.shape[-1]
    far = stored - NEAR
    shifts = shift_radius.shape[0]
    two_nvec = start_block.shape[2]
    cols = shifts * two_nvec
    meta = plan(columns, counts, me, n)
    chips = n // 2
    far_rows = (n - 1) * HB
    far_pairs, near_pairs = pair_counts(slots, far, n)
    flops = ITERS * 4 * slots * stored * width * width * cols
    smem = pl.BlockSpec(memory_space=pltpu.SMEM)
    hbm = pl.BlockSpec(memory_space=pl.ANY)
    return pl.pallas_call(
        functools.partial(kernel, n, slots, far, two_nvec // 2, shifts),
        out_shape=pltpu.VMEM((slots, 2, cols, width), F32),
        in_specs=[smem, smem, smem, hbm, hbm],
        out_specs=pl.BlockSpec(memory_space=pltpu.VMEM),
        scratch_shapes=[
            pltpu.VMEM((slots + 1, NEAR, width, width), BF16),
            pltpu.VMEM((slots + 1, far, width, width), BF16),
            pltpu.VMEM((slots, stored * width, width), BF16),
            pltpu.VMEM((2 * shifts, two_nvec // 2, width), F32),
            pltpu.VMEM(start_block.shape, F32),
            pltpu.VMEM((2, slots + 1, cols, width), BF16),
            pltpu.VMEM((2, slots, cols, width), BF16),
            pltpu.VMEM((near_pairs + 1, cols, width), F32),
            pltpu.VMEM((far_pairs + 1, cols, width), F32),
            pltpu.VMEM((chips * HB, cols, width), F32),
            pltpu.VMEM((2, chips * HB, cols, width), F32),
            pltpu.VMEM(((chips - 1) * HB, cols, width), BF16),
            pltpu.VMEM((2, far_rows, cols, width), BF16),
            pltpu.VMEM((far_rows, cols, width), BF16),
            pltpu.VMEM((2, (chips - 1) * HB, cols, width), BF16),
            pltpu.SemaphoreType.DMA((1,)),
            pltpu.SemaphoreType.DMA((slots // pick_unroll(slots, 8),)),
            pltpu.SemaphoreType.DMA((slots // pick_unroll(slots, 8),)),
            pltpu.SemaphoreType.DMA((chips,)),
            pltpu.SemaphoreType.DMA((2, chips)),
            pltpu.SemaphoreType.DMA((chips - 1,)),
            pltpu.SemaphoreType.DMA((2, chips - 1)),
            pltpu.SemaphoreType.DMA((1,)),
            pltpu.SemaphoreType.DMA((2,)),
            pltpu.SemaphoreType.DMA((chips - 1,)),
            pltpu.SemaphoreType.DMA((2, chips - 1)),
        ],
        compiler_params=pltpu.CompilerParams(
            collective_id=0, has_side_effects=True, vmem_limit_bytes=54 * 1024 * 1024
        ),
        cost_estimate=pl.CostEstimate(
            flops=flops, bytes_accessed=2 * blocks.size, transcendentals=0
        ),
    )(meta, shift_radius, shift_angle, blocks, start_block)


def solution(mesh):
    placed = (
        P("rows", None, None, None),
        P("rows", None),
        P("rows"),
        P("rows", None, None, None),
        P("dom"),
        P("dom"),
    )
    return jax.shard_map(
        body,
        mesh=mesh,
        in_specs=placed,
        out_specs=P(("dom", "rows"), None, None, None),
        check_vma=False,
    )
```

```python
import functools

import jax
import jax.numpy as jnp
from jax import lax
from jax.experimental import pallas as pl
from jax.experimental.pallas import tpu as pltpu
from jax.sharding import PartitionSpec as P

HB = 2
ITERS = 4
NEAR = 4
F32 = jnp.float32
BF16 = jnp.bfloat16


def pick_unroll(total, want):
    while total % want:
        want -= 1
    return want


def pair_counts(slots, far, n):
    far_rows = (n - 1) * HB
    far_pairs = (slots * far + far_rows) // 2
    near_pairs = (slots * NEAR + slots) // 2
    return -(-far_pairs // 8) * 8, -(-near_pairs // 8) * 8


def split(entry, width):
    if width & (width - 1):
        k = lax.div(entry, jnp.int32(width))
        return k, entry - k * width
    shift = width.bit_length() - 1
    return lax.shift_right_logical(entry, jnp.int32(shift)), entry & (width - 1)


def kernel(
    n, slots, far, nvec, shifts,
    meta, radius, angle, blocks, start, out,
    near_w, far_w, turned, weight, drive, upper, lower, near_sum, far_sum,
    pair_out, pair_in, send_terms, heads, far_heads, terms,
    load_sem, far_sem, near_sem, head_send, head_recv, pass_send, pass_recv,
    pair_send, pair_recv, term_send, term_recv,
):
    me = lax.axis_index("rows")
    near_total = slots * (NEAR - 1)
    far_total = slots * far
    far_rows = (n - 1) * HB
    far_pairs, near_pairs = pair_counts(slots, far, n)
    chips = n // 2
    core = lax.rem(me, 2)
    chip = me // 2

    def partner(off):
        if off == 0:
            return chip * 2 + 1 - core
        return lax.rem(chip + off, chips) * 2 + core

    at_keep = 2 * (far_pairs + near_pairs)
    at_far_last = at_keep + far_pairs + near_pairs
    at_near_last = at_far_last + far_rows
    at_near_col = at_near_last + slots
    at_far_col = at_near_col + near_total
    at_count = at_far_col + far_total

    load_start = pltpu.make_async_copy(start, drive, load_sem.at[0])
    chunk = pick_unroll(slots, 8)
    width = turned.shape[2]

    def load_far(i):
        rows = pl.ds(i * chunk, chunk)
        return pltpu.make_async_copy(blocks.at[rows, NEAR:], far_w.at[rows], far_sem.at[i])

    def load_near(i):
        rows = pl.ds(i * chunk, chunk)
        return pltpu.make_async_copy(blocks.at[rows, :NEAR], near_w.at[rows], near_sem.at[i])

    load_start.start()
    for i in range(slots // chunk):
        load_far(i).start()
        load_near(i).start()

    barrier = pltpu.get_barrier_semaphore()
    for off in range(chips):
        pl.semaphore_signal(
            barrier, inc=1, device_id={"rows": partner(off)},
            device_id_type=pl.DeviceIdType.MESH,
        )

    def rotated(values):
        pieces = []
        for s in range(shifts):
            re = values[(2 * s) * nvec:(2 * s + 1) * nvec]
            im = values[(2 * s + 1) * nvec:(2 * s + 2) * nvec]
            w_re = weight[s]
            w_im = weight[shifts + s]
            pieces.append(w_re * re - w_im * im)
            pieces.append(w_re * im + w_im * re)
        return jnp.concatenate(pieces, 0)

    def driven(k, half):
        return jnp.concatenate([drive[k, half]] * shifts, 0)

    for s in range(shifts):
        turn_by = jnp.full(weight.shape[1:], angle[s], F32)
        size = jnp.full(weight.shape[1:], radius[s], F32)
        weight[s] = jnp.cos(turn_by) / size
        weight[shifts + s] = -jnp.sin(turn_by) / size
    load_start.wait()

    def begin(k, carry):
        alive = (k < meta[at_count]).astype(F32)
        drive[k] = drive[k] * alive
        upper[0, k] = rotated(driven(k, 0)).astype(BF16)
        lower[0, k] = rotated(driven(k, 1)).astype(BF16)
        return carry

    lax.fori_loop(0, slots, begin, 0, unroll=8)
    for p in range(2):
        upper[p, slots] = jnp.zeros(upper.shape[2:], upper.dtype)
    near_w[slots, 0] = jnp.zeros(near_w.shape[2:], near_w.dtype)
    far_w[slots, 0] = jnp.zeros(far_w.shape[2:], far_w.dtype)
    near_sum[0] = jnp.zeros(near_sum.shape[1:], near_sum.dtype)
    far_sum[0] = jnp.zeros(far_sum.shape[1:], far_sum.dtype)
    pl.semaphore_wait(barrier, chips)

    def send(source, target, send_sem, recv_sem, off):
        return pltpu.make_async_remote_copy(
            src_ref=source, dst_ref=target, send_sem=send_sem, recv_sem=recv_sem,
            device_id={"rows": partner(off)}, device_id_type=pl.DeviceIdType.MESH,
        )

    def head_copy(p, off):
        there = 0 if off == 0 else 2 * (chips - off) - 1
        return send(
            lower.at[p, pl.ds(0, HB)], heads.at[p, pl.ds(there * HB, HB)],
            head_send.at[off], head_recv.at[p, 0 if off == 0 else chips - off], off,
        )

    def pass_copy(p, off):
        return send(
            heads.at[p, pl.ds((2 * off - 1) * HB, HB)], heads.at[p, pl.ds(2 * off * HB, HB)],
            pass_send.at[off - 1], pass_recv.at[p, off - 1], 0,
        )

    def pair_copy(p):
        return send(pair_out, pair_in.at[p], pair_send.at[0], pair_recv.at[p], 0)

    def term_copy(p, off):
        return send(
            send_terms.at[pl.ds((off - 1) * HB, HB)],
            terms.at[p, pl.ds((chips - off - 1) * HB, HB)],
            term_send.at[off - 1], term_recv.at[p, chips - off - 1], off,
        )

    def dot(a, b):
        return jnp.dot(a, b, preferred_element_type=F32)

    def sweep(s, last):
        p = lax.rem(s, 2)
        q = 1 - p
        for off in range(1, chips):
            head_copy(p, off).start()
        head_copy(p, 0).start()

        zero = jnp.zeros(upper.shape[2:], F32)

        def running(first, low, high, acc, blocks_of, weights, sums):
            step = pick_unroll(high - low, 80)
            group = pick_unroll(step, 8)

            def go(i, acc):
                for g in range(step // group):
                    found = []
                    for u in range(group):
                        j = low + i * step + g * group + u
                        lhs, rhs = [], []
                        for side in range(2):
                            e = meta[2 * (first + j) + side]
                            k, c = split(e, blocks_of)
                            lhs.append(upper[p, k])
                            rhs.append(weights[k, c])
                        found.append(dot(jnp.concatenate(lhs, 1), jnp.concatenate(rhs, 0)))
                    for u in range(group):
                        j = low + i * step + g * group + u
                        acc = acc * meta[at_keep + first + j].astype(F32) + found[u]
                        sums[j + 1] = acc.astype(sums.dtype)
                return acc

            return lax.fori_loop(0, (high - low) // step, go, acc)

        running(0, 0, far_pairs, zero, far, far_w, far_sum)
        for off in range(chips):
            for h in range(HB):
                row = 2 * off * HB + h
                pair_out[off * HB + h] = far_sum[meta[at_far_last + row]]
        pair_copy(p).start()
        half = near_pairs // 2
        acc = running(far_pairs, 0, half, zero, NEAR, near_w, near_sum)
        pair_copy(p).wait_recv()
        for off in range(1, chips):
            for h in range(HB):
                row = (2 * off - 1) * HB + h
                send_terms[(off - 1) * HB + h] = (
                    far_sum[meta[at_far_last + row]] + pair_in[p, off * HB + h]
                ).astype(BF16)
            term_copy(p, off).start()
        for off in range(1, chips):
            head_copy(p, chips - off).wait_recv()
            pass_copy(p, off).start()
        running(far_pairs, half, near_pairs, acc, NEAR, near_w, near_sum)

        def bottom(k, extra):
            value = driven(k, 1) + near_sum[meta[at_near_last + k]]
            if extra:
                value = value + pair_in[p, k]
                for off in range(chips - 1):
                    value = value + terms[p, off * HB + k].astype(F32)
            value = rotated(value)
            if last:
                out[k, 1] = value
            else:
                lower[q, k] = value.astype(BF16)

        def bottom_step(k, carry):
            bottom(k, False)
            return carry

        lax.fori_loop(HB, slots, bottom_step, 0, unroll=pick_unroll(slots - HB, 31))

        head_copy(p, 0).wait_recv()
        for off in range(1, chips):
            pass_copy(p, off).wait_recv()
        for row in range(far_rows):
            far_heads[row] = heads[p, row]

        step_top = pick_unroll(slots, 32)
        group_top = pick_unroll(step_top, 4)

        def top_step(i, carry):
            for g in range(step_top // group_top):
                found = []
                for u in range(group_top):
                    k = i * step_top + g * group_top + u
                    tiles = [lower[p, k]]
                    for c in range(NEAR - 1):
                        tiles.append(lower[p, meta[at_near_col + k * (NEAR - 1) + c]])
                    for c in range(far):
                        tiles.append(far_heads[meta[at_far_col + k * far + c]])
                    found.append(dot(jnp.concatenate(tiles, 1), turned[k]))
                for u in range(group_top):
                    k = i * step_top + g * group_top + u
                    alive = (k < meta[at_count]).astype(F32)
                    value = rotated(driven(k, 0) + found[u] * alive)
                    if last:
                        out[k, 0] = value
                    else:
                        upper[q, k] = value.astype(BF16)
            return carry

        lax.fori_loop(0, slots // step_top, top_step, 0)

        for off in range(1, chips):
            term_copy(p, off).wait_recv()
        for k in range(HB):
            bottom(k, True)
        pair_copy(p).wait_send()
        for off in range(chips):
            head_copy(p, off).wait_send()
        for off in range(1, chips):
            pass_copy(p, off).wait_send()
            term_copy(p, off).wait_send()


    def turn(i, carry):
        load_far(i).wait()
        load_near(i).wait()
        for u in range(chunk):
            k = i * chunk + u
            for c in range(NEAR + far):
                block = near_w[k, c] if c < NEAR else far_w[k, c - NEAR]
                turned[k, c * width:(c + 1) * width] = block.T
        return carry

    lax.fori_loop(0, slots // chunk, turn, 0)

    def middle(s, carry):
        sweep(s, False)
        return carry

    lax.fori_loop(0, ITERS - 1, middle, 0)
    sweep(ITERS - 1, True)


def store(source, out, sems):
    parts = sems.shape[0]
    rows = source.shape[0] // parts
    copies = []
    for i in range(parts):
        part = pl.ds(i * rows, rows)
        copies.append(pltpu.make_async_copy(source.at[part], out.at[part], sems.at[i]))
    for copy in copies:
        copy.start()
    for copy in copies:
        copy.wait()


def plan(columns, counts, me, n):
    slots, stored = columns.shape
    far = stored - NEAR
    owner = columns // slots
    within = columns - owner * slots
    chips = n // 2
    rel = 2 * lax.rem(owner // 2 - me // 2 + chips, chips) + lax.rem(owner + me, 2)
    far_rows = (n - 1) * HB
    far_pairs, near_pairs = pair_counts(slots, far, n)
    near_all = within[:, :NEAR].reshape(-1)
    far_col = jnp.clip((rel - 1) * HB + within, 0, far_rows - 1)[:, NEAR:].reshape(-1)
    far_total = far_col.shape[0]
    dest = jnp.concatenate([far_col, far_rows + near_all])
    here = jnp.arange(dest.shape[0], dtype=jnp.int32)
    entry = jnp.where(here < far_total, here, here - far_total)
    rows = jnp.arange(far_rows + slots, dtype=jnp.int32)
    same = dest[None, :] == dest[:, None]
    order = jnp.sum((same & (here[None, :] < here[:, None])).astype(jnp.int32), 1)
    even = 1 - (order & 1)
    is_near = (rows >= far_rows).astype(jnp.int32)
    dest_near = (dest >= far_rows).astype(jnp.int32)
    ahead_rows = is_near * far_pairs + jnp.sum(
        jnp.where((dest[None, :] < rows[:, None]) & (dest_near[None, :] == is_near[:, None]),
                  even[None, :], 0), 1)
    own_rows = jnp.sum(jnp.where(dest[None, :] == rows[:, None], even[None, :], 0), 1)
    ahead = dest_near * far_pairs + jnp.sum(
        jnp.where((dest[None, :] < dest[:, None]) & (dest_near[None, :] == dest_near[:, None]),
                  even[None, :], 0), 1)
    place = 2 * ahead + order
    pairs = far_pairs + near_pairs
    spots = jnp.arange(2 * pairs, dtype=jnp.int32)
    empty = jnp.where(spots < 2 * far_pairs, slots * far, slots * NEAR)
    listed = jnp.sum(
        jnp.where(place[None, :] == spots[:, None], entry[None, :] - empty[:, None], 0), 1
    ) + empty
    pair_ids = jnp.arange(pairs, dtype=jnp.int32)
    starts = (ahead_rows[None, :] == pair_ids[:, None]) & (own_rows[None, :] > 0)
    keep = 1 - jnp.sum(starts.astype(jnp.int32), 1)
    ends = jnp.where(own_rows > 0, ahead_rows + own_rows - is_near * far_pairs, 0)
    return jnp.concatenate(
        [listed, keep, ends, within[:, 1:NEAR].reshape(-1), far_col, counts]
    )


def body(blocks, columns, counts, start_block, shift_radius, shift_angle):
    me = lax.axis_index("rows")
    n = lax.axis_size("rows")
    slots, stored, width = blocks.shape[0], blocks.shape[1], blocks.shape[-1]
    far = stored - NEAR
    shifts = shift_radius.shape[0]
    two_nvec = start_block.shape[2]
    cols = shifts * two_nvec
    meta = plan(columns, counts, me, n)
    chips = n // 2
    far_rows = (n - 1) * HB
    far_pairs, near_pairs = pair_counts(slots, far, n)
    flops = ITERS * 4 * slots * stored * width * width * cols
    smem = pl.BlockSpec(memory_space=pltpu.SMEM)
    hbm = pl.BlockSpec(memory_space=pl.ANY)
    found = pl.pallas_call(
        functools.partial(kernel, n, slots, far, two_nvec // 2, shifts),
        out_shape=pltpu.VMEM((slots, 2, cols, width), F32),
        in_specs=[smem, smem, smem, hbm, hbm],
        out_specs=pl.BlockSpec(memory_space=pltpu.VMEM),
        scratch_shapes=[
            pltpu.VMEM((slots + 1, NEAR, width, width), BF16),
            pltpu.VMEM((slots + 1, far, width, width), BF16),
            pltpu.VMEM((slots, stored * width, width), BF16),
            pltpu.VMEM((2 * shifts, two_nvec // 2, width), F32),
            pltpu.VMEM(start_block.shape, F32),
            pltpu.VMEM((2, slots + 1, cols, width), BF16),
            pltpu.VMEM((2, slots, cols, width), BF16),
            pltpu.VMEM((near_pairs + 1, cols, width), F32),
            pltpu.VMEM((far_pairs + 1, cols, width), F32),
            pltpu.VMEM((chips * HB, cols, width), F32),
            pltpu.VMEM((2, chips * HB, cols, width), F32),
            pltpu.VMEM(((chips - 1) * HB, cols, width), BF16),
            pltpu.VMEM((2, far_rows, cols, width), BF16),
            pltpu.VMEM((far_rows, cols, width), BF16),
            pltpu.VMEM((2, (chips - 1) * HB, cols, width), BF16),
            pltpu.SemaphoreType.DMA((1,)),
            pltpu.SemaphoreType.DMA((slots // pick_unroll(slots, 8),)),
            pltpu.SemaphoreType.DMA((slots // pick_unroll(slots, 8),)),
            pltpu.SemaphoreType.DMA((chips,)),
            pltpu.SemaphoreType.DMA((2, chips)),
            pltpu.SemaphoreType.DMA((chips - 1,)),
            pltpu.SemaphoreType.DMA((2, chips - 1)),
            pltpu.SemaphoreType.DMA((1,)),
            pltpu.SemaphoreType.DMA((2,)),
            pltpu.SemaphoreType.DMA((chips - 1,)),
            pltpu.SemaphoreType.DMA((2, chips - 1)),
        ],
        compiler_params=pltpu.CompilerParams(
            collective_id=0, has_side_effects=True, vmem_limit_bytes=54 * 1024 * 1024
        ),
        cost_estimate=pl.CostEstimate(
            flops=flops, bytes_accessed=2 * blocks.size, transcendentals=0
        ),
    )(meta, shift_radius, shift_angle, blocks, start_block)
    return pl.pallas_call(
        store,
        out_shape=jax.ShapeDtypeStruct(found.shape, F32),
        in_specs=[pl.BlockSpec(memory_space=pltpu.VMEM)],
        out_specs=hbm,
        scratch_shapes=[pltpu.SemaphoreType.DMA((pick_unroll(slots, 8),))],
        compiler_params=pltpu.CompilerParams(vmem_limit_bytes=8 * 1024 * 1024),
    )(found)


def solution(mesh):
    placed = (
        P("rows", None, None, None),
        P("rows", None),
        P("rows"),
        P("rows", None, None, None),
        P("dom"),
        P("dom"),
    )
    return jax.shard_map(
        body,
        mesh=mesh,
        in_specs=placed,
        out_specs=P(("dom", "rows"), None, None, None),
        check_vma=False,
    )
```

```python
import functools

import jax
import jax.numpy as jnp
from jax import lax
from jax.experimental import pallas as pl
from jax.experimental.pallas import tpu as pltpu
from jax.sharding import PartitionSpec as P

HB = 2
ITERS = 4
NEAR = 4
F32 = jnp.float32
BF16 = jnp.bfloat16


def pick_unroll(total, want):
    while total % want:
        want -= 1
    return want


def pair_counts(slots, far, n):
    far_rows = (n - 1) * HB
    far_pairs = (slots * far + far_rows) // 2
    near_pairs = (slots * NEAR + slots) // 2
    return -(-far_pairs // 8) * 8, -(-near_pairs // 8) * 8


def split(entry, width):
    if width & (width - 1):
        k = lax.div(entry, jnp.int32(width))
        return k, entry - k * width
    shift = width.bit_length() - 1
    return lax.shift_right_logical(entry, jnp.int32(shift)), entry & (width - 1)


def kernel(
    n, slots, far, nvec, shifts,
    meta, radius, angle, blocks, start, out,
    near_w, far_w, turned, weight, drive, upper, lower, near_sum, far_sum,
    pair_out, pair_in, send_terms, heads, far_heads, terms,
    load_sem, far_sem, near_sem, head_send, head_recv, pass_send, pass_recv,
    pair_send, pair_recv, term_send, term_recv,
):
    me = lax.axis_index("rows")
    near_total = slots * (NEAR - 1)
    far_total = slots * far
    far_rows = (n - 1) * HB
    far_pairs, near_pairs = pair_counts(slots, far, n)
    chips = n // 2
    core = lax.rem(me, 2)
    chip = me // 2

    def partner(off):
        if off == 0:
            return chip * 2 + 1 - core
        return lax.rem(chip + off, chips) * 2 + core

    at_keep = 2 * (far_pairs + near_pairs)
    at_far_last = at_keep + far_pairs + near_pairs
    at_near_last = at_far_last + far_rows
    at_near_col = at_near_last + slots
    at_far_col = at_near_col + near_total
    at_count = at_far_col + far_total

    load_start = pltpu.make_async_copy(start, drive, load_sem.at[0])
    chunk = pick_unroll(slots, 8)
    width = turned.shape[2]

    def load_far(i):
        rows = pl.ds(i * chunk, chunk)
        return pltpu.make_async_copy(blocks.at[rows, NEAR:], far_w.at[rows], far_sem.at[i])

    def load_near(i):
        rows = pl.ds(i * chunk, chunk)
        return pltpu.make_async_copy(blocks.at[rows, :NEAR], near_w.at[rows], near_sem.at[i])

    load_start.start()
    for i in range(slots // chunk):
        load_far(i).start()
    for i in range(slots // chunk):
        load_near(i).start()

    barrier = pltpu.get_barrier_semaphore()
    for off in range(chips):
        pl.semaphore_signal(
            barrier, inc=1, device_id={"rows": partner(off)},
            device_id_type=pl.DeviceIdType.MESH,
        )

    def rotated(values):
        pieces = []
        for s in range(shifts):
            re = values[(2 * s) * nvec:(2 * s + 1) * nvec]
            im = values[(2 * s + 1) * nvec:(2 * s + 2) * nvec]
            w_re = weight[s]
            w_im = weight[shifts + s]
            pieces.append(w_re * re - w_im * im)
            pieces.append(w_re * im + w_im * re)
        return jnp.concatenate(pieces, 0)

    def driven(k, half):
        return jnp.concatenate([drive[k, half]] * shifts, 0)

    for s in range(shifts):
        turn_by = jnp.full(weight.shape[1:], angle[s], F32)
        size = jnp.full(weight.shape[1:], radius[s], F32)
        weight[s] = jnp.cos(turn_by) / size
        weight[shifts + s] = -jnp.sin(turn_by) / size
    load_start.wait()

    def begin(k, carry):
        alive = (k < meta[at_count]).astype(F32)
        drive[k] = drive[k] * alive
        upper[0, k] = rotated(driven(k, 0)).astype(BF16)
        lower[0, k] = rotated(driven(k, 1)).astype(BF16)
        return carry

    lax.fori_loop(0, slots, begin, 0, unroll=8)
    for p in range(2):
        upper[p, slots] = jnp.zeros(upper.shape[2:], upper.dtype)
    near_w[slots, 0] = jnp.zeros(near_w.shape[2:], near_w.dtype)
    far_w[slots, 0] = jnp.zeros(far_w.shape[2:], far_w.dtype)
    near_sum[0] = jnp.zeros(near_sum.shape[1:], near_sum.dtype)
    far_sum[0] = jnp.zeros(far_sum.shape[1:], far_sum.dtype)
    pl.semaphore_wait(barrier, chips)

    def send(source, target, send_sem, recv_sem, off):
        return pltpu.make_async_remote_copy(
            src_ref=source, dst_ref=target, send_sem=send_sem, recv_sem=recv_sem,
            device_id={"rows": partner(off)}, device_id_type=pl.DeviceIdType.MESH,
        )

    def head_copy(p, off):
        there = 0 if off == 0 else 2 * (chips - off) - 1
        return send(
            lower.at[p, pl.ds(0, HB)], heads.at[p, pl.ds(there * HB, HB)],
            head_send.at[off], head_recv.at[p, 0 if off == 0 else chips - off], off,
        )

    def pass_copy(p, off):
        return send(
            heads.at[p, pl.ds((2 * off - 1) * HB, HB)], heads.at[p, pl.ds(2 * off * HB, HB)],
            pass_send.at[off - 1], pass_recv.at[p, off - 1], 0,
        )

    def pair_copy(p):
        return send(pair_out, pair_in.at[p], pair_send.at[0], pair_recv.at[p], 0)

    def term_copy(p, off):
        return send(
            send_terms.at[pl.ds((off - 1) * HB, HB)],
            terms.at[p, pl.ds((chips - off - 1) * HB, HB)],
            term_send.at[off - 1], term_recv.at[p, chips - off - 1], off,
        )

    def dot(a, b):
        return jnp.dot(a, b, preferred_element_type=F32)

    def sweep(s, last, first):
        p = s % 2 if isinstance(s, int) else lax.rem(s, 2)
        q = 1 - p
        for off in range(1, chips):
            head_copy(p, off).start()
        head_copy(p, 0).start()

        zero = jnp.zeros(upper.shape[2:], F32)

        def running(first, low, high, acc, blocks_of, weights, sums):
            step = pick_unroll(high - low, 80)
            group = pick_unroll(step, 8)

            def go(i, acc):
                for g in range(step // group):
                    found = []
                    for u in range(group):
                        j = low + i * step + g * group + u
                        lhs, rhs = [], []
                        for side in range(2):
                            e = meta[2 * (first + j) + side]
                            k, c = split(e, blocks_of)
                            lhs.append(upper[p, k])
                            rhs.append(weights[k, c])
                        found.append(dot(jnp.concatenate(lhs, 1), jnp.concatenate(rhs, 0)))
                    for u in range(group):
                        j = low + i * step + g * group + u
                        acc = acc * meta[at_keep + first + j].astype(F32) + found[u]
                        sums[j + 1] = acc.astype(sums.dtype)
                return acc

            return lax.fori_loop(0, (high - low) // step, go, acc)

        if first:
            for i in range(slots // chunk):
                load_far(i).wait()
        running(0, 0, far_pairs, zero, far, far_w, far_sum)
        for off in range(chips):
            for h in range(HB):
                row = 2 * off * HB + h
                pair_out[off * HB + h] = far_sum[meta[at_far_last + row]]
        pair_copy(p).start()
        half = near_pairs // 2
        if first:
            for i in range(slots // chunk):
                load_near(i).wait()
        acc = running(far_pairs, 0, half, zero, NEAR, near_w, near_sum)
        pair_copy(p).wait_recv()
        for off in range(1, chips):
            for h in range(HB):
                row = (2 * off - 1) * HB + h
                send_terms[(off - 1) * HB + h] = (
                    far_sum[meta[at_far_last + row]] + pair_in[p, off * HB + h]
                ).astype(BF16)
            term_copy(p, off).start()
        for off in range(1, chips):
            head_copy(p, chips - off).wait_recv()
            pass_copy(p, off).start()
        running(far_pairs, half, near_pairs, acc, NEAR, near_w, near_sum)

        def bottom(k, extra):
            value = driven(k, 1) + near_sum[meta[at_near_last + k]]
            if extra:
                value = value + pair_in[p, k]
                for off in range(chips - 1):
                    value = value + terms[p, off * HB + k].astype(F32)
            value = rotated(value)
            if last:
                out[k, 1] = value
            else:
                lower[q, k] = value.astype(BF16)

        def bottom_step(k, carry):
            bottom(k, False)
            return carry

        lax.fori_loop(HB, slots, bottom_step, 0, unroll=pick_unroll(slots - HB, 31))

        head_copy(p, 0).wait_recv()
        for off in range(1, chips):
            pass_copy(p, off).wait_recv()
        for row in range(far_rows):
            far_heads[row] = heads[p, row]

        step_top = pick_unroll(slots, 16 if first else 32)
        group_top = pick_unroll(step_top, 4)

        def top_step(i, carry):
            for g in range(step_top // group_top):
                found = []
                for u in range(group_top):
                    k = i * step_top + g * group_top + u
                    tiles = [lower[p, k]]
                    for c in range(NEAR - 1):
                        tiles.append(lower[p, meta[at_near_col + k * (NEAR - 1) + c]])
                    for c in range(far):
                        tiles.append(far_heads[meta[at_far_col + k * far + c]])
                    if first:
                        for c in range(NEAR + far):
                            block = near_w[k, c] if c < NEAR else far_w[k, c - NEAR]
                            turned[k, c * width:(c + 1) * width] = block.T
                    found.append(dot(jnp.concatenate(tiles, 1), turned[k]))
                for u in range(group_top):
                    k = i * step_top + g * group_top + u
                    alive = (k < meta[at_count]).astype(F32)
                    value = rotated(driven(k, 0) + found[u] * alive)
                    if last:
                        out[k, 0] = value
                    else:
                        upper[q, k] = value.astype(BF16)
            return carry

        lax.fori_loop(0, slots // step_top, top_step, 0)

        for off in range(1, chips):
            term_copy(p, off).wait_recv()
        for k in range(HB):
            bottom(k, True)
        pair_copy(p).wait_send()
        for off in range(chips):
            head_copy(p, off).wait_send()
        for off in range(1, chips):
            pass_copy(p, off).wait_send()
            term_copy(p, off).wait_send()


    def middle(s, carry):
        sweep(s, False, False)
        return carry

    sweep(0, ITERS == 1, True)
    if ITERS > 1:
        lax.fori_loop(1, ITERS - 1, middle, 0)
        sweep(ITERS - 1, True, False)


def store(source, out, sems):
    parts = sems.shape[0]
    rows = source.shape[0] // parts
    copies = []
    for i in range(parts):
        part = pl.ds(i * rows, rows)
        copies.append(pltpu.make_async_copy(source.at[part], out.at[part], sems.at[i]))
    for copy in copies:
        copy.start()
    for copy in copies:
        copy.wait()


def plan(columns, counts, me, n):
    slots, stored = columns.shape
    far = stored - NEAR
    owner = columns // slots
    within = columns - owner * slots
    chips = n // 2
    rel = 2 * lax.rem(owner // 2 - me // 2 + chips, chips) + lax.rem(owner + me, 2)
    far_rows = (n - 1) * HB
    far_pairs, near_pairs = pair_counts(slots, far, n)
    near_all = within[:, :NEAR].reshape(-1)
    far_col = jnp.clip((rel - 1) * HB + within, 0, far_rows - 1)[:, NEAR:].reshape(-1)
    far_total = far_col.shape[0]
    dest = jnp.concatenate([far_col, far_rows + near_all])
    here = jnp.arange(dest.shape[0], dtype=jnp.int32)
    entry = jnp.where(here < far_total, here, here - far_total)
    rows = jnp.arange(far_rows + slots, dtype=jnp.int32)
    same = dest[None, :] == dest[:, None]
    order = jnp.sum((same & (here[None, :] < here[:, None])).astype(jnp.int32), 1)
    even = 1 - (order & 1)
    is_near = (rows >= far_rows).astype(jnp.int32)
    dest_near = (dest >= far_rows).astype(jnp.int32)
    ahead_rows = is_near * far_pairs + jnp.sum(
        jnp.where((dest[None, :] < rows[:, None]) & (dest_near[None, :] == is_near[:, None]),
                  even[None, :], 0), 1)
    own_rows = jnp.sum(jnp.where(dest[None, :] == rows[:, None], even[None, :], 0), 1)
    ahead = dest_near * far_pairs + jnp.sum(
        jnp.where((dest[None, :] < dest[:, None]) & (dest_near[None, :] == dest_near[:, None]),
                  even[None, :], 0), 1)
    place = 2 * ahead + order
    pairs = far_pairs + near_pairs
    spots = jnp.arange(2 * pairs, dtype=jnp.int32)
    empty = jnp.where(spots < 2 * far_pairs, slots * far, slots * NEAR)
    listed = jnp.sum(
        jnp.where(place[None, :] == spots[:, None], entry[None, :] - empty[:, None], 0), 1
    ) + empty
    pair_ids = jnp.arange(pairs, dtype=jnp.int32)
    starts = (ahead_rows[None, :] == pair_ids[:, None]) & (own_rows[None, :] > 0)
    keep = 1 - jnp.sum(starts.astype(jnp.int32), 1)
    ends = jnp.where(own_rows > 0, ahead_rows + own_rows - is_near * far_pairs, 0)
    return jnp.concatenate(
        [listed, keep, ends, within[:, 1:NEAR].reshape(-1), far_col, counts]
    )


def body(blocks, columns, counts, start_block, shift_radius, shift_angle):
    me = lax.axis_index("rows")
    n = lax.axis_size("rows")
    slots, stored, width = blocks.shape[0], blocks.shape[1], blocks.shape[-1]
    far = stored - NEAR
    shifts = shift_radius.shape[0]
    two_nvec = start_block.shape[2]
    cols = shifts * two_nvec
    meta = plan(columns, counts, me, n)
    chips = n // 2
    far_rows = (n - 1) * HB
    far_pairs, near_pairs = pair_counts(slots, far, n)
    flops = ITERS * 4 * slots * stored * width * width * cols
    smem = pl.BlockSpec(memory_space=pltpu.SMEM)
    hbm = pl.BlockSpec(memory_space=pl.ANY)
    found = pl.pallas_call(
        functools.partial(kernel, n, slots, far, two_nvec // 2, shifts),
        out_shape=pltpu.VMEM((slots, 2, cols, width), F32),
        in_specs=[smem, smem, smem, hbm, hbm],
        out_specs=pl.BlockSpec(memory_space=pltpu.VMEM),
        scratch_shapes=[
            pltpu.VMEM((slots + 1, NEAR, width, width), BF16),
            pltpu.VMEM((slots + 1, far, width, width), BF16),
            pltpu.VMEM((slots, stored * width, width), BF16),
            pltpu.VMEM((2 * shifts, two_nvec // 2, width), F32),
            pltpu.VMEM(start_block.shape, F32),
            pltpu.VMEM((2, slots + 1, cols, width), BF16),
            pltpu.VMEM((2, slots, cols, width), BF16),
            pltpu.VMEM((near_pairs + 1, cols, width), F32),
            pltpu.VMEM((far_pairs + 1, cols, width), F32),
            pltpu.VMEM((chips * HB, cols, width), F32),
            pltpu.VMEM((2, chips * HB, cols, width), F32),
            pltpu.VMEM(((chips - 1) * HB, cols, width), BF16),
            pltpu.VMEM((2, far_rows, cols, width), BF16),
            pltpu.VMEM((far_rows, cols, width), BF16),
            pltpu.VMEM((2, (chips - 1) * HB, cols, width), BF16),
            pltpu.SemaphoreType.DMA((1,)),
            pltpu.SemaphoreType.DMA((slots // pick_unroll(slots, 8),)),
            pltpu.SemaphoreType.DMA((slots // pick_unroll(slots, 8),)),
            pltpu.SemaphoreType.DMA((chips,)),
            pltpu.SemaphoreType.DMA((2, chips)),
            pltpu.SemaphoreType.DMA((chips - 1,)),
            pltpu.SemaphoreType.DMA((2, chips - 1)),
            pltpu.SemaphoreType.DMA((1,)),
            pltpu.SemaphoreType.DMA((2,)),
            pltpu.SemaphoreType.DMA((chips - 1,)),
            pltpu.SemaphoreType.DMA((2, chips - 1)),
        ],
        compiler_params=pltpu.CompilerParams(
            collective_id=0, has_side_effects=True, vmem_limit_bytes=54 * 1024 * 1024
        ),
        cost_estimate=pl.CostEstimate(
            flops=flops, bytes_accessed=2 * blocks.size, transcendentals=0
        ),
    )(meta, shift_radius, shift_angle, blocks, start_block)
    return pl.pallas_call(
        store,
        out_shape=jax.ShapeDtypeStruct(found.shape, F32),
        in_specs=[pl.BlockSpec(memory_space=pltpu.VMEM)],
        out_specs=hbm,
        scratch_shapes=[pltpu.SemaphoreType.DMA((pick_unroll(slots, 8),))],
        compiler_params=pltpu.CompilerParams(vmem_limit_bytes=8 * 1024 * 1024),
    )(found)


def solution(mesh):
    placed = (
        P("rows", None, None, None),
        P("rows", None),
        P("rows"),
        P("rows", None, None, None),
        P("dom"),
        P("dom"),
    )
    return jax.shard_map(
        body,
        mesh=mesh,
        in_specs=placed,
        out_specs=P(("dom", "rows"), None, None, None),
        check_vma=False,
    )
```
